32 devices in a mesh: gx: 4 (over x, core), gy: 4 (over z), gz: 2 (over y).
Axes of the slice: x: 2, y: 2, z: 4, core: 2. Of those that a mesh axis runs over, the one named last changes fastest.
Arguments:
- body_force: float32 [3, 16, 32, 512], P(None, 'gz', 'gx', 'gy'), may hold values from -6 to 6
- viscosity: float32 [16, 32, 512], P('gz', 'gx', 'gy'), may hold values from 0.05 to 0.5
- topography: float32 [256, 4096], P('gx', 'gy'), may hold values from -6 to 6
- kappa: bfloat16 [256, 4096], P('gx', 'gy'), may hold values from 0.019897461 to 0.19921875
Outputs:
- velocity: float32 [3, 16, 32, 512], P(None, 'gz', 'gx', 'gy')
- surface: float32 [256, 4096], P('gx', ('gy', 'gz'))
The draws below stay inside these ranges and needn't reach their ends.
All inputs are finite; a program needn't handle non-finite values.
Results may differ from the reference program's by a relative error of at most 0.0008.
Values may be sent and summed in bfloat16 or wider, within the bound.
A program may use at most 64 MiB of HBM per device.

```python
import math
import jax
import jax.numpy as jnp

ITERS = 2
STEPS = 8
FR = 8
FC = 8
NX = 32
NY = 512
NZ = 16
NR = 256
NC = 4096


def level_of(stream_key, dims, pieces, least, largest):
    gain = 1.0
    for dim, parts in pieces:
        draws = jax.random.uniform(jax.random.fold_in(jax.random.fold_in(stream_key, 6), dim), (parts,), jnp.float32, least / len(pieces), largest / len(pieces))
        gain = gain * jnp.repeat(jnp.exp(draws), dims[dim] // parts).reshape((-1,) + (1,) * (len(dims) - 1 - dim))
    return gain


def noise(own_key, dims, width, limit, shards=(), kind=jnp.bfloat16):
    drawn = jax.random.normal(own_key, dims, jnp.float32) * width
    if len(shards) > 0:
        drawn = level_of(own_key, dims, shards, -0.22, 0.18) * drawn
    return jnp.clip(drawn, min=-limit, max=limit).astype(kind)


def setup_inputs(seed: int = 0) -> dict:
    keys = jax.random.split(jax.random.key(seed), 5)
    return {
        "body_force": noise(keys[0], (3, NZ, NX, NY), 1.0, 6.0, ((1, 2), (2, 4), (3, 4)), jnp.float32),
        "viscosity": jnp.clip(jnp.exp(math.log(0.5) - 2.3025851 * jax.random.uniform(keys[1], (NZ, NX, NY), jnp.float32) ** level_of(keys[1], (NZ, NX, NY), ((0, 2), (1, 4), (2, 4)), -0.2, 0.2)), 0.05, 0.5),
        "topography": noise(keys[2], (NR, NC), 1.0, 6.0, ((0, 4), (1, 4)), jnp.float32),
        "kappa": jnp.clip(jnp.exp(math.log(0.19921875) - 2.3038113 * jax.random.uniform(keys[3], (NR, NC), jnp.float32) ** level_of(keys[3], (NR, NC), ((0, 4), (1, 4)), -0.2, 0.2)), 0.019897461, 0.19921875).astype(jnp.bfloat16),
    }


drag = 1.0
time_step = 1.0
load_gain = 4.0

def shifts():
    found = []
    for depth in (-1, 0, 1):
        for across in (-1, 0, 1):
            for along in (-1, 0, 1):
                if depth != 0 or across != 0 or along != 0:
                    found.append((depth, across, along))
    return found

def window(array, depth, across, along):
    inner_depth = array.shape[-3] - 2
    inner_rows = array.shape[-2] - 2
    inner_cols = array.shape[-1] - 2
    return array[..., 1 + depth:1 + depth + inner_depth, 1 + across:1 + across + inner_rows, 1 + along:1 + along + inner_cols]

def apply_operator(padded, viscous):
    center = window(padded, 0, 0, 0)
    eta_center = window(viscous, 0, 0, 0)
    total = drag * center
    for depth, across, along in shifts():
        weight = 0.5 / (depth * depth + across * across + along * along)
        coupling = weight * (eta_center + window(viscous, depth, across, along))
        total = total + coupling * (center - window(padded, depth, across, along))
    return total

def pad_cells(field):
    return jnp.pad(field, ((0, 0), (1, 1), (1, 1), (1, 1)))

def flux(slope, conduct):
    return conduct * slope / jnp.sqrt(1.0 + slope * slope)

def diffuse_step(extended, conduct):
    along = flux(extended[:, 1:] - extended[:, :-1], 0.5 * (conduct[:, 1:] + conduct[:, :-1]))
    across = flux(extended[1:, :] - extended[:-1, :], 0.5 * (conduct[1:, :] + conduct[:-1, :]))
    change = along[1:-1, 1:] - along[1:-1, :-1] + across[1:, 1:-1] - across[:-1, 1:-1]
    return extended[1:-1, 1:-1] + time_step * change

def reference(body_force, viscosity, topography, kappa):
    load = topography.reshape(NX, FR, NY, FC).mean(axis=(1, 3))
    force = body_force.at[2, NZ - 1].add(-load_gain * load)
    viscous = pad_cells(viscosity[None])
    velocity = jnp.zeros_like(force)
    residual = force
    direction = force
    norm_now = jnp.sum(residual * residual)
    for step in range(ITERS):
        image = apply_operator(pad_cells(direction), viscous)
        alpha = norm_now / jnp.sum(direction * image)
        velocity = velocity + alpha * direction
        if step + 1 < ITERS:
            residual = residual - alpha * image
            norm_next = jnp.sum(residual * residual)
            direction = residual + norm_next / norm_now * direction
            norm_now = norm_next
    top = velocity[2, NZ - 1]
    rise = jnp.broadcast_to(top[:, None, :, None], (NX, FR, NY, FC)).reshape(NR, NC)
    conduct = jnp.pad(kappa.astype(jnp.float32), 1)
    height = topography
    for step in range(STEPS):
        height = diffuse_step(jnp.pad(height, 1), conduct)
    surface = height + STEPS * time_step * rise
    return (velocity, surface)
```

```python
import functools

import jax
import jax.numpy as jnp
from jax import lax
from jax.experimental import pallas as pl
from jax.experimental.pallas import tpu as pltpu
from jax.sharding import PartitionSpec as P

STEPS = 8
REACH = 2

drag = 1.0
time_step = 1.0
load_gain = 4.0

W_FACE = 0.5
W_EDGE = 0.25
W_CORNER = 0.5 / 3.0
W_ALL = 6 * W_FACE + 12 * W_EDGE + 8 * W_CORNER

MESH = pl.DeviceIdType.MESH
HIGH = lax.Precision.HIGHEST
SIGNS = (-1, 0, 1)
OFFSETS = [(a, b, c) for a in SIGNS for b in SIGNS for c in SIGNS if (a, b, c) != (0, 0, 0)]


def side(sign):
    return 0 if sign < 0 else 1


def code(a, b, c):
    return (a + 1) * 9 + (b + 1) * 3 + (c + 1)


def weighted(u):
    rows, lanes = u.shape[1:]
    beside = pltpu.roll(u, 1, 2) + pltpu.roll(u, lanes - 1, 2)
    near = beside + pltpu.roll(u, 1, 1) + pltpu.roll(u, rows - 1, 1)
    diagonal = pltpu.roll(beside, 1, 1) + pltpu.roll(beside, rows - 1, 1)
    same = W_FACE * near + W_EDGE * diagonal
    other = W_FACE * u + W_EDGE * near + W_CORNER * diagonal
    return same[1:-1] + other[:-2] + other[2:]


def total(x):
    x = x.reshape((-1,) + x.shape[-2:]).sum(axis=0)
    return x.sum(axis=(0, 1), keepdims=True)


def kernel(
    sizes,
    force_hbm,
    visc_hbm,
    topo_hbm,
    kappa_hbm,
    velocity_ref,
    surface_ref,
    field,
    lane_pack,
    row_pack,
    from_depth,
    from_rows,
    from_rows_depth,
    from_cols,
    ext,
    image,
    height,
    conduct,
    work,
    face_right,
    face_down,
    inside,
    row_out,
    gathered,
    top_own,
    top_in,
    load_sem,
    rim_send,
    rim_recv,
    surf_send,
    surf_recv,
    sum_send,
    sum_recv,
    top_send,
    top_recv,
):
    nx, ny, nz = sizes
    count = nx * ny * nz
    x, y, z = lax.axis_index("gx"), lax.axis_index("gy"), lax.axis_index("gz")
    depth, cells, width = field.shape[1:]
    rows, cols = topo_hbm.shape
    share = cols // nz
    krow = 16

    xs = [lax.rem(x + k, nx) for k in range(nx)]
    ys = [lax.rem(y + k, ny) for k in range(ny)]
    zs = [lax.rem(z + k, nz) for k in range(nz)]
    others = [(a, b, c) for a in range(nx) for b in range(ny) for c in range(nz)][1:]
    others.sort(key=lambda o: -(min(o[0], nx - o[0]) + min(o[1], ny - o[1]) + min(o[2], nz - o[2])))
    is_top = z == nz - 1

    loads = [
        pltpu.make_async_copy(topo_hbm, height.at[STEPS : STEPS + rows, width : width + cols], load_sem.at[0]),
        pltpu.make_async_copy(force_hbm, field.at[0:3], load_sem.at[1]),
        pltpu.make_async_copy(visc_hbm, field.at[3], load_sem.at[2]),
        pltpu.make_async_copy(kappa_hbm, conduct.at[krow : krow + rows, width : width + cols], load_sem.at[3]),
    ]
    for copy in loads:
        copy.start()

    for ref in (from_depth, from_rows, from_rows_depth, from_cols):
        ref[...] = jnp.zeros_like(ref)
    height[0:STEPS, :] = jnp.zeros((STEPS, height.shape[1]), height.dtype)
    height[STEPS + rows :, :] = jnp.zeros((STEPS, height.shape[1]), height.dtype)
    height[STEPS : STEPS + rows, 0:width] = jnp.zeros((rows, width), height.dtype)
    height[STEPS : STEPS + rows, width + cols :] = jnp.zeros((rows, width), height.dtype)
    conduct[0:krow, :] = jnp.zeros((krow, conduct.shape[1]), conduct.dtype)
    conduct[krow + rows :, :] = jnp.zeros((krow, conduct.shape[1]), conduct.dtype)
    conduct[krow : krow + rows, 0:width] = jnp.zeros((rows, width), conduct.dtype)
    conduct[krow : krow + rows, width + cols :] = jnp.zeros((rows, width), conduct.dtype)

    barrier = pltpu.get_barrier_semaphore()
    for a, b, c in others:
        pl.semaphore_signal(barrier, inc=1, device_id=(xs[a], ys[b], zs[c]), device_id_type=MESH)

    loads[0].wait()
    ratio_r, ratio_c = rows // cells, cols // width
    by_rows = height[STEPS : STEPS + rows, width : width + cols].reshape(cells, ratio_r, cols).sum(axis=1)
    at = lax.broadcasted_iota(jnp.int32, (cols, width), 0)
    first = lax.broadcasted_iota(jnp.int32, (cols, width), 1) * ratio_c
    pick = jnp.where((at >= first) & (at < first + ratio_c), 1.0, 0.0)
    load = jnp.dot(by_rows, pick, precision=HIGH, preferred_element_type=jnp.float32) / (ratio_r * ratio_c)
    loads[1].wait()
    loads[2].wait()
    field[2, depth - 1] = field[2, depth - 1] + jnp.where(is_top, -load_gain * load, 0.0)

    lane = lax.broadcasted_iota(jnp.int32, (cells, width), 1)
    sub = lax.broadcasted_iota(jnp.int32, (cells, width), 0)
    packed = jnp.zeros((cells, width), jnp.float32)
    up_pack, down_pack = {}, {}
    for f in range(4):
        for d in range(depth):
            tile = field[f, d]
            j = f * depth + d
            packed = jnp.where((lane >= 4 * j) & (lane < 4 * j + 4), pltpu.roll(tile, (4 * j + 2) % width, 1), packed)
            t, p = (d // 2) * 2 + f // 2, (d % 2) * 2 + f % 2
            chosen = (sub >= 2 * p) & (sub < 2 * p + 2)
            up = pltpu.roll(tile, (2 * p) % 8, 0) if p else tile
            down = pltpu.roll(tile, (2 * p + 2) % 8, 0) if (2 * p + 2) % 8 else tile
            up_pack[t] = jnp.where(chosen, up, up_pack.get(t, 0.0))
            down_pack[t] = jnp.where(chosen, down, down_pack.get(t, 0.0))
    lane_pack[...] = packed
    for t in range(depth):
        row_pack[0, t] = up_pack[t]
        row_pack[1, t] = down_pack[t]

    def present(a, b, c):
        yes = None
        for sign, at_, size in ((a, z, nz), (b, x, nx), (c, y, ny)):
            if sign:
                one = at_ > 0 if sign < 0 else at_ < size - 1
                yes = one if yes is None else jnp.logical_and(yes, one)
        return yes

    def rim_copy(a, b, c):
        span = slice(depth - 2, depth) if a > 0 else slice(0, 2)
        if c != 0:
            src, dst = lane_pack, from_cols.at[(1 - a) * 3 + (1 - b), side(-c)]
        elif b == 0:
            src, dst = field.at[:, span], from_depth.at[side(-a)]
        elif a == 0:
            src, dst = row_pack.at[side(b)], from_rows.at[side(-b)]
        else:
            src, dst = row_pack.at[side(b), span], from_rows_depth.at[side(-a), side(-b)]
        return pltpu.make_async_remote_copy(
            src_ref=src,
            dst_ref=dst,
            send_sem=rim_send.at[code(a, b, c)],
            recv_sem=rim_recv.at[code(-a, -b, -c)],
            device_id=(x + b, y + c, z + a),
            device_id_type=MESH,
        )

    pl.semaphore_wait(barrier, count - 1)
    for o in OFFSETS:
        pl.when(present(*o))(lambda o=o: rim_copy(*o).start())

    surf_offsets = [(b, c) for b in SIGNS for c in SIGNS if (b, c) != (0, 0)]

    def surf_present(b, c, receiving):
        yes = present(0, b, c)
        toward = -c if receiving else c
        if toward > 0:
            yes = jnp.logical_and(yes, z == 0)
        if toward < 0:
            yes = jnp.logical_and(yes, z == nz - 1)
        return yes

    def surf_copies(b, c):
        def spans(sign, size, halo, lead):
            if sign == 0:
                return slice(0, size), slice(lead, lead + size)
            if sign > 0:
                return slice(size - halo, size), slice(0, halo)
            return slice(0, halo), slice(lead + size, lead + size + halo)

        cs, cd = spans(c, cols, width, width)
        n = (b + 1) * 3 + (c + 1)
        m = (1 - b) * 3 + (1 - c)
        made = []
        for i, (src, dst, halo) in enumerate(((topo_hbm, height, STEPS), (kappa_hbm, conduct, krow))):
            rs, rd = spans(b, rows, halo, halo)
            made.append(
                pltpu.make_async_remote_copy(
                    src_ref=src.at[rs, cs],
                    dst_ref=dst.at[rd, cd],
                    send_sem=surf_send.at[i, n],
                    recv_sem=surf_recv.at[i, m],
                    device_id=(x + b, y + c, z),
                    device_id_type=MESH,
                )
            )
        return made

    def surf_start(b, c):
        for copy in surf_copies(b, c):
            copy.start()

    for o in surf_offsets:
        pl.when(surf_present(*o, False))(lambda o=o: surf_start(*o))

    for a, b, c in OFFSETS:
        pl.when(present(a, b, c))(lambda o=(-a, -b, -c): rim_copy(*o).wait_recv())
    from_low = sub < cells // 2
    from_left = (lane % 4) < 2
    for a in SIGNS:
        joined = []
        low = from_cols[(a + 1) * 3 + 1, 0]
        high = from_cols[(a + 1) * 3 + 1, 1]
        if True:
            joined.append(jnp.where(from_left, low, high))
            low = jnp.where(from_low, from_cols[(a + 1) * 3 + 2, 0], from_cols[(a + 1) * 3, 0])
            high = jnp.where(from_low, from_cols[(a + 1) * 3 + 2, 1], from_cols[(a + 1) * 3, 1])
            joined.append(jnp.where(from_left, low, high))
        for f in range(4):
            for d in range(depth) if a == 0 else (range(2) if a > 0 else range(depth - 2, depth)):
                layer = REACH + a * depth + d
                t, p = (d // 2) * 2 + f // 2, (d % 2) * 2 + f % 2
                if a == 0:
                    center, above, below = field[f, d], from_rows[0, t], from_rows[1, t]
                else:
                    center = from_depth[side(a), f, d % 2]
                    above = from_rows_depth[side(a), 0, f // 2]
                    below = from_rows_depth[side(a), 1, f // 2]
                above = pltpu.roll(above, 6 - 2 * p, 0) if p != 3 else above
                below = pltpu.roll(below, 8 - 2 * p, 0) if p else below
                j = f * depth + d
                ext[f, layer, 0:cells, 0:width] = center
                ext[f, layer, cells:, 0:width] = jnp.where(from_low, below, above)
                turn = (width - 2 - 4 * j) % width
                for r in range(2):
                    tile = pltpu.roll(joined[r], turn, 1) if turn else joined[r]
                    ext[f, layer, r * cells : (r + 1) * cells, width:] = tile

    eta = ext[3]
    gain = drag + W_ALL * eta[1:-1] + weighted(eta)
    for f in range(3):
        v = ext[f]
        out = gain * v[1:-1] - eta[1:-1] * weighted(v) - weighted(eta * v)
        image[f] = jnp.where(eta[1:-1] > 0.0, out, 0.0)
    eta1 = eta[1:-1]
    center = (slice(None), slice(0, cells), slice(0, width))
    m0 = m1 = jnp.zeros((cells, width), jnp.float32)
    for f in range(3):
        b = field[f]
        ab = image[f, 1:-1, 0:cells, 0:width]
        m0 = m0 + (b * b).sum(axis=0)
        m1 = m1 + (b * ab).sum(axis=0)
    m0, m1 = total(m0), total(m1)
    own = jnp.where(m0 > 0.0, m1 / m0, 0.0)
    sums = [jnp.zeros((cells, width), jnp.float32) for _ in range(4)]
    for f in range(3):
        v = image[f]
        b = field[f]
        ab = v[1:-1][center]
        again = (
            gain[1:-1][center] * ab
            - eta1[1:-1][center] * weighted(v)[center]
            - weighted(eta1 * v)[center]
        )
        w = ab - own * b
        aw = again - own * ab
        for i, (p, q) in enumerate(((w, b), (w, w), (w, aw), (b, aw))):
            sums[i] = sums[i] + (p * q).sum(axis=0)
    numbers = [m0, m1, own] + [total(s) for s in sums]
    spot = lax.broadcasted_iota(jnp.int32, (1, width), 1)
    line = jnp.zeros((1, width), jnp.float32)
    for i, number in enumerate(numbers):
        line = jnp.where(spot == i, number, line)
    row_out[0] = line
    me = (x * ny + y) * nz + z
    gathered[me] = line
    top_own[0] = field[2, depth - 1]
    top_own[1] = image[2, depth, 0:cells, 0:width]
    for a, b, c in others:
        pltpu.make_async_remote_copy(
            src_ref=row_out.at[0],
            dst_ref=gathered.at[me],
            send_sem=sum_send,
            recv_sem=sum_recv,
            device_id=(xs[a], ys[b], zs[c]),
            device_id_type=MESH,
        ).start()

    def top_copy(k):
        return pltpu.make_async_remote_copy(
            src_ref=top_own,
            dst_ref=top_in,
            send_sem=top_send.at[k],
            recv_sem=top_recv,
            device_id=(x, y, zs[k]),
            device_id_type=MESH,
        )

    @pl.when(is_top)
    def _():
        for k in range(1, nz):
            top_copy(k).start()

    for b, c in surf_offsets:

        def arrived(b=b, c=c):
            for copy in surf_copies(-b, -c):
                copy.wait_recv()

        pl.when(surf_present(b, c, True))(arrived)
    loads[3].wait()
    start = pl.multiple_of(z * share, share)
    tall = rows + 2 * STEPS
    left_half = lax.broadcasted_iota(jnp.int32, (1, width), 1) < width // 2

    def joined_window(ref):
        wide = ref[:, pl.ds(start, share + 2 * width)].astype(jnp.float32)
        rim = jnp.where(left_half, wide[:, width + share :], wide[:, :width])
        return jnp.concatenate([wide[:, width : width + share], rim], axis=1)

    work[...] = joined_window(height)
    k = joined_window(conduct)[krow - STEPS : krow + rows + STEPS]
    span = share + width
    face_right[...] = 0.5 * (k + pltpu.roll(k, span - 1, 1))
    face_down[...] = 0.5 * (k + pltpu.roll(k, tall - 1, 0))
    row_at = x * rows - STEPS + lax.broadcasted_iota(jnp.int32, (tall, span), 0)
    lane_at = lax.broadcasted_iota(jnp.int32, (tall, span), 1)
    lane_at = jnp.where(lane_at >= span - width // 2, lane_at - span, lane_at)
    col_at = y * cols + z * share + lane_at
    inside[...] = jnp.where(
        (row_at >= 0) & (row_at < rows * nx) & (col_at >= 0) & (col_at < cols * ny), time_step, 0.0
    )

    def diffuse(_, carry):
        h = work[...]
        s = pltpu.roll(h, span - 1, 1) - h
        along = face_right[...] * s * lax.rsqrt(1.0 + s * s)
        s = pltpu.roll(h, tall - 1, 0) - h
        across = face_down[...] * s * lax.rsqrt(1.0 + s * s)
        change = along - pltpu.roll(along, 1, 1) + across - pltpu.roll(across, 1, 0)
        work[...] = h + inside[...] * change
        return carry

    lax.fori_loop(0, STEPS, diffuse, 0)

    @pl.when(jnp.logical_not(is_top))
    def _():
        top_copy(1).wait_recv()
        top_own[...] = top_in[...]

    cell_at = lax.broadcasted_iota(jnp.int32, (width, share), 0) * ratio_c
    col = z * share + lax.broadcasted_iota(jnp.int32, (width, share), 1)
    pick = jnp.where((col >= cell_at) & (col < cell_at + ratio_c), 1.0, 0.0)
    spread = jnp.dot(
        top_own[...].reshape(2 * cells, width), pick, precision=HIGH, preferred_element_type=jnp.float32
    )

    for o in OFFSETS:
        pl.when(present(*o))(lambda o=o: rim_copy(*o).wait_send())
    for b, c in surf_offsets:

        def sent(b=b, c=c):
            for copy in surf_copies(b, c):
                copy.wait_send()

        pl.when(surf_present(b, c, False))(sent)

    @pl.when(is_top)
    def _():
        for k in range(1, nz):
            top_copy(k).wait_send()

    most = gathered.at[pl.ds(0, count - 1)]
    pltpu.make_async_copy(most, most, sum_send).wait()
    pltpu.make_async_copy(most, most, sum_recv).wait()

    table = gathered[...].reshape(count, width)
    m0, m1, own, e, ww, waw, baw = [table[:, i : i + 1] for i in range(7)]
    rr = m0.sum(axis=0, keepdims=True)
    bab = m1.sum(axis=0, keepdims=True)
    mean = bab / rr
    off = own - mean
    s2 = (ww + off * (2.0 * e + off * m0)).sum(axis=0, keepdims=True)
    q = (waw + off * (ww + own * e + baw + off * m1)).sum(axis=0, keepdims=True)
    alpha0 = rr / bab
    beta = s2 / (mean * bab)
    alpha1 = s2 / (q - s2 * s2 / bab)
    on_b = alpha0 + alpha1 * (1.0 + beta)
    on_ab = -alpha1 * alpha0
    for f in range(3):
        velocity_ref[f] = on_b * field[f] + on_ab * image[f, 1:-1, 0:cells, 0:width]
    rise = (STEPS * time_step) * (on_b * spread[:cells] + on_ab * spread[cells:])
    rise = jnp.broadcast_to(rise[:, None, :], (cells, ratio_r, share)).reshape(rows, share)
    surface_ref[...] = work[STEPS : STEPS + rows, 0:share] + rise


def local(sizes, body_force, viscosity, topography, kappa):
    depth, cells, width = viscosity.shape
    rows, cols = topography.shape
    nx, ny, nz = sizes
    count = nx * ny * nz
    share = cols // nz
    f32 = jnp.float32
    dma = pltpu.SemaphoreType.DMA
    return pl.pallas_call(
        functools.partial(kernel, sizes),
        out_shape=(
            jax.ShapeDtypeStruct(body_force.shape, f32),
            jax.ShapeDtypeStruct((rows, share), f32),
        ),
        in_specs=[pl.BlockSpec(memory_space=pl.ANY)] * 4,
        out_specs=[pl.BlockSpec(memory_space=pltpu.VMEM)] * 2,
        scratch_shapes=[
            pltpu.VMEM((4, depth, cells, width), f32),
            pltpu.VMEM((cells, width), f32),
            pltpu.VMEM((2, depth, cells, width), f32),
            pltpu.VMEM((2, 4, REACH, cells, width), f32),
            pltpu.VMEM((2, depth, cells, width), f32),
            pltpu.VMEM((2, 2, 2, cells, width), f32),
            pltpu.VMEM((9, 2, cells, width), f32),
            pltpu.VMEM((4, depth + 2 * REACH, 2 * cells, 2 * width), f32),
            pltpu.VMEM((3, depth + 2 * REACH - 2, 2 * cells, 2 * width), f32),
            pltpu.VMEM((rows + 2 * STEPS, cols + 2 * width), f32),
            pltpu.VMEM((rows + 32, cols + 2 * width), kappa.dtype),
            pltpu.VMEM((rows + 2 * STEPS, share + width), f32),
            pltpu.VMEM((rows + 2 * STEPS, share + width), f32),
            pltpu.VMEM((rows + 2 * STEPS, share + width), f32),
            pltpu.VMEM((rows + 2 * STEPS, share + width), f32),
            pltpu.VMEM((1, 1, width), f32),
            pltpu.VMEM((count, 1, width), f32),
            pltpu.VMEM((2, cells, width), f32),
            pltpu.VMEM((2, cells, width), f32),
            dma((4,)),
            dma((27,)),
            dma((27,)),
            dma((2, 9)),
            dma((2, 9)),
            dma,
            dma,
            dma((nz,)),
            dma,
        ],
        compiler_params=pltpu.CompilerParams(
            collective_id=0, has_side_effects=True, vmem_limit_bytes=32 * 1024 * 1024
        ),
    )(body_force, viscosity, topography, kappa)


def solution(mesh):
    sizes = tuple(mesh.shape[axis] for axis in ("gx", "gy", "gz"))
    in_specs = (P(None, "gz", "gx", "gy"), P("gz", "gx", "gy"), P("gx", "gy"), P("gx", "gy"))
    out_specs = (P(None, "gz", "gx", "gy"), P("gx", ("gy", "gz")))
    return jax.shard_map(
        functools.partial(local, sizes), mesh=mesh, in_specs=in_specs, out_specs=out_specs, check_vma=False
    )
```

```python
import functools

import jax
import jax.numpy as jnp
from jax import lax
from jax.experimental import pallas as pl
from jax.experimental.pallas import tpu as pltpu
from jax.sharding import PartitionSpec as P

STEPS = 8
REACH = 2

drag = 1.0
time_step = 1.0
load_gain = 4.0

W_FACE = 0.5
W_EDGE = 0.25
W_CORNER = 0.5 / 3.0
W_ALL = 6 * W_FACE + 12 * W_EDGE + 8 * W_CORNER

MESH = pl.DeviceIdType.MESH
SIGNS = (-1, 0, 1)
OFFSETS = [(a, b, c) for a in SIGNS for b in SIGNS for c in SIGNS if (a, b, c) != (0, 0, 0)]


def side(sign):
    return 0 if sign < 0 else 1


def code(a, b, c):
    return (a + 1) * 9 + (b + 1) * 3 + (c + 1)


def weighted(u):
    rows, lanes = u.shape[1:]
    beside = pltpu.roll(u, 1, 2) + pltpu.roll(u, lanes - 1, 2)
    near = beside + pltpu.roll(u, 1, 1) + pltpu.roll(u, rows - 1, 1)
    diagonal = pltpu.roll(beside, 1, 1) + pltpu.roll(beside, rows - 1, 1)
    same = W_FACE * near + W_EDGE * diagonal
    other = W_FACE * u + W_EDGE * near + W_CORNER * diagonal
    return same[1:-1] + other[:-2] + other[2:]


def picked(x, choice):
    parts = []
    for _ in range(3):
        part = x.astype(jnp.bfloat16)
        parts.append(part.astype(jnp.float32))
        x = x - parts[-1]
    rows = x.shape[0]
    stacked = jnp.concatenate(parts, axis=0).astype(jnp.bfloat16)
    out = jnp.dot(stacked, choice, preferred_element_type=jnp.float32)
    return out[:rows] + (out[rows : 2 * rows] + out[2 * rows :])


def total(x):
    x = x.reshape((-1,) + x.shape[-2:]).sum(axis=0)
    return x.sum(axis=(0, 1), keepdims=True)


def kernel(
    sizes,
    force_hbm,
    visc_hbm,
    topo_hbm,
    kappa_hbm,
    velocity_ref,
    surface_ref,
    field,
    lane_pack,
    row_pack,
    from_depth,
    from_rows,
    from_rows_depth,
    from_cols,
    ext,
    image,
    height,
    conduct,
    work,
    face_right,
    face_down,
    inside,
    row_out,
    gathered,
    top_own,
    top_in,
    load_sem,
    rim_send,
    rim_recv,
    surf_send,
    surf_recv,
    sum_send,
    sum_recv,
    top_send,
    top_recv,
):
    nx, ny, nz = sizes
    count = nx * ny * nz
    x, y, z = lax.axis_index("gx"), lax.axis_index("gy"), lax.axis_index("gz")
    depth, cells, width = field.shape[1:]
    rows, cols = topo_hbm.shape
    share = cols // nz
    krow = 16

    xs = [lax.rem(x + k, nx) for k in range(nx)]
    ys = [lax.rem(y + k, ny) for k in range(ny)]
    zs = [lax.rem(z + k, nz) for k in range(nz)]
    others = [(a, b, c) for a in range(nx) for b in range(ny) for c in range(nz)][1:]
    others.sort(key=lambda o: -(min(o[0], nx - o[0]) + min(o[1], ny - o[1]) + min(o[2], nz - o[2])))
    is_top = z == nz - 1

    loads = [
        pltpu.make_async_copy(topo_hbm, height.at[STEPS : STEPS + rows, width : width + cols], load_sem.at[0]),
        pltpu.make_async_copy(force_hbm, field.at[0:3], load_sem.at[1]),
        pltpu.make_async_copy(visc_hbm, field.at[3], load_sem.at[2]),
        pltpu.make_async_copy(kappa_hbm, conduct.at[krow : krow + rows, width : width + cols], load_sem.at[3]),
    ]
    for copy in loads:
        copy.start()

    for ref in (from_depth, from_rows, from_rows_depth, from_cols):
        ref[...] = jnp.zeros_like(ref)
    height[0:STEPS, :] = jnp.zeros((STEPS, height.shape[1]), height.dtype)
    height[STEPS + rows :, :] = jnp.zeros((STEPS, height.shape[1]), height.dtype)
    height[STEPS : STEPS + rows, 0:width] = jnp.zeros((rows, width), height.dtype)
    height[STEPS : STEPS + rows, width + cols :] = jnp.zeros((rows, width), height.dtype)
    conduct[0:krow, :] = jnp.zeros((krow, conduct.shape[1]), conduct.dtype)
    conduct[krow + rows :, :] = jnp.zeros((krow, conduct.shape[1]), conduct.dtype)
    conduct[krow : krow + rows, 0:width] = jnp.zeros((rows, width), conduct.dtype)
    conduct[krow : krow + rows, width + cols :] = jnp.zeros((rows, width), conduct.dtype)

    barrier = pltpu.get_barrier_semaphore()
    for a, b, c in others:
        pl.semaphore_signal(barrier, inc=1, device_id=(xs[a], ys[b], zs[c]), device_id_type=MESH)

    loads[0].wait()
    ratio_r, ratio_c = rows // cells, cols // width
    by_rows = height[STEPS : STEPS + rows, width : width + cols].reshape(cells, ratio_r, cols).sum(axis=1)
    at = lax.broadcasted_iota(jnp.int32, (cols, width), 0)
    first = lax.broadcasted_iota(jnp.int32, (cols, width), 1) * ratio_c
    pick = jnp.where((at >= first) & (at < first + ratio_c), 1.0, 0.0)
    load = picked(by_rows, pick.astype(jnp.bfloat16)) * (1.0 / (ratio_r * ratio_c))
    loads[1].wait()
    loads[2].wait()
    field[2, depth - 1] = field[2, depth - 1] + jnp.where(is_top, -load_gain * load, 0.0)

    lane = lax.broadcasted_iota(jnp.int32, (cells, width), 1)
    sub = lax.broadcasted_iota(jnp.int32, (cells, width), 0)
    packed = jnp.zeros((cells, width), jnp.float32)
    up_pack, down_pack = {}, {}
    for f in range(4):
        for d in range(depth):
            tile = field[f, d]
            j = f * depth + d
            packed = jnp.where((lane >= 4 * j) & (lane < 4 * j + 4), pltpu.roll(tile, (4 * j + 2) % width, 1), packed)
            t, p = (d // 2) * 2 + f // 2, (d % 2) * 2 + f % 2
            chosen = (sub >= 2 * p) & (sub < 2 * p + 2)
            up = pltpu.roll(tile, (2 * p) % 8, 0) if p else tile
            down = pltpu.roll(tile, (2 * p + 2) % 8, 0) if (2 * p + 2) % 8 else tile
            up_pack[t] = jnp.where(chosen, up, up_pack.get(t, 0.0))
            down_pack[t] = jnp.where(chosen, down, down_pack.get(t, 0.0))
    lane_pack[...] = packed
    for t in range(depth):
        row_pack[0, t] = up_pack[t]
        row_pack[1, t] = down_pack[t]

    def present(a, b, c):
        yes = None
        for sign, at_, size in ((a, z, nz), (b, x, nx), (c, y, ny)):
            if sign:
                one = at_ > 0 if sign < 0 else at_ < size - 1
                yes = one if yes is None else jnp.logical_and(yes, one)
        return yes

    def rim_copy(a, b, c):
        span = slice(depth - 2, depth) if a > 0 else slice(0, 2)
        if c != 0:
            src, dst = lane_pack, from_cols.at[(1 - a) * 3 + (1 - b), side(-c)]
        elif b == 0:
            src, dst = field.at[:, span], from_depth.at[side(-a)]
        elif a == 0:
            src, dst = row_pack.at[side(b)], from_rows.at[side(-b)]
        else:
            src, dst = row_pack.at[side(b), span], from_rows_depth.at[side(-a), side(-b)]
        return pltpu.make_async_remote_copy(
            src_ref=src,
            dst_ref=dst,
            send_sem=rim_send.at[code(a, b, c)],
            recv_sem=rim_recv.at[code(-a, -b, -c)],
            device_id=(x + b, y + c, z + a),
            device_id_type=MESH,
        )

    pl.semaphore_wait(barrier, count - 1)
    for o in OFFSETS:
        pl.when(present(*o))(lambda o=o: rim_copy(*o).start())

    surf_offsets = [(b, c) for b in SIGNS for c in SIGNS if (b, c) != (0, 0)]

    def surf_present(b, c, receiving):
        yes = present(0, b, c)
        toward = -c if receiving else c
        if toward > 0:
            yes = jnp.logical_and(yes, z == 0)
        if toward < 0:
            yes = jnp.logical_and(yes, z == nz - 1)
        return yes

    def surf_copies(b, c):
        def spans(sign, size, halo, lead):
            if sign == 0:
                return slice(0, size), slice(lead, lead + size)
            if sign > 0:
                return slice(size - halo, size), slice(0, halo)
            return slice(0, halo), slice(lead + size, lead + size + halo)

        cs, cd = spans(c, cols, width, width)
        n = (b + 1) * 3 + (c + 1)
        m = (1 - b) * 3 + (1 - c)
        made = []
        for i, (src, dst, halo) in enumerate(((topo_hbm, height, STEPS), (kappa_hbm, conduct, krow))):
            rs, rd = spans(b, rows, halo, halo)
            made.append(
                pltpu.make_async_remote_copy(
                    src_ref=src.at[rs, cs],
                    dst_ref=dst.at[rd, cd],
                    send_sem=surf_send.at[i, n],
                    recv_sem=surf_recv.at[i, m],
                    device_id=(x + b, y + c, z),
                    device_id_type=MESH,
                )
            )
        return made

    def surf_start(b, c):
        for copy in surf_copies(b, c):
            copy.start()

    for o in surf_offsets:
        pl.when(surf_present(*o, False))(lambda o=o: surf_start(*o))

    for a, b, c in OFFSETS:
        pl.when(present(a, b, c))(lambda o=(-a, -b, -c): rim_copy(*o).wait_recv())
    from_low = sub < cells // 2
    from_left = (lane % 4) < 2
    for a in SIGNS:
        joined = []
        low = from_cols[(a + 1) * 3 + 1, 0]
        high = from_cols[(a + 1) * 3 + 1, 1]
        if True:
            joined.append(jnp.where(from_left, low, high))
            low = jnp.where(from_low, from_cols[(a + 1) * 3 + 2, 0], from_cols[(a + 1) * 3, 0])
            high = jnp.where(from_low, from_cols[(a + 1) * 3 + 2, 1], from_cols[(a + 1) * 3, 1])
            joined.append(jnp.where(from_left, low, high))
        for f in range(4):
            for d in range(depth) if a == 0 else (range(2) if a > 0 else range(depth - 2, depth)):
                layer = REACH + a * depth + d
                t, p = (d // 2) * 2 + f // 2, (d % 2) * 2 + f % 2
                if a == 0:
                    center, above, below = field[f, d], from_rows[0, t], from_rows[1, t]
                else:
                    center = from_depth[side(a), f, d % 2]
                    above = from_rows_depth[side(a), 0, f // 2]
                    below = from_rows_depth[side(a), 1, f // 2]
                above = pltpu.roll(above, 6 - 2 * p, 0) if p != 3 else above
                below = pltpu.roll(below, 8 - 2 * p, 0) if p else below
                j = f * depth + d
                ext[f, layer, 0:cells, 0:width] = center
                ext[f, layer, cells:, 0:width] = jnp.where(from_low, below, above)
                turn = (width - 2 - 4 * j) % width
                for r in range(2):
                    tile = pltpu.roll(joined[r], turn, 1) if turn else joined[r]
                    ext[f, layer, r * cells : (r + 1) * cells, width:] = tile

    eta = ext[3]
    gain = drag + W_ALL * eta[1:-1] + weighted(eta)
    for f in range(3):
        v = ext[f]
        out = gain * v[1:-1] - eta[1:-1] * weighted(v) - weighted(eta * v)
        image[f] = jnp.where(eta[1:-1] > 0.0, out, 0.0)
    eta1 = eta[1:-1]
    center = (slice(None), slice(0, cells), slice(0, width))
    m0 = m1 = jnp.zeros((cells, width), jnp.float32)
    for f in range(3):
        b = field[f]
        ab = image[f, 1:-1, 0:cells, 0:width]
        m0 = m0 + (b * b).sum(axis=0)
        m1 = m1 + (b * ab).sum(axis=0)
    m0, m1 = total(m0), total(m1)
    own = jnp.where(m0 > 0.0, m1 / m0, 0.0)
    sums = [jnp.zeros((cells, width), jnp.float32) for _ in range(4)]
    for f in range(3):
        v = image[f]
        b = field[f]
        ab = v[1:-1][center]
        again = (
            gain[1:-1][center] * ab
            - eta1[1:-1][center] * weighted(v)[center]
            - weighted(eta1 * v)[center]
        )
        w = ab - own * b
        aw = again - own * ab
        for i, (p, q) in enumerate(((w, b), (w, w), (w, aw), (b, aw))):
            sums[i] = sums[i] + (p * q).sum(axis=0)
    numbers = [m0, m1, own] + [total(s) for s in sums]
    spot = lax.broadcasted_iota(jnp.int32, (1, width), 1)
    line = jnp.zeros((1, width), jnp.float32)
    for i, number in enumerate(numbers):
        line = jnp.where(spot == i, number, line)
    row_out[0] = line
    me = (x * ny + y) * nz + z
    gathered[me] = line
    top_own[0] = field[2, depth - 1]
    top_own[1] = image[2, depth, 0:cells, 0:width]
    for a, b, c in others:
        pltpu.make_async_remote_copy(
            src_ref=row_out.at[0],
            dst_ref=gathered.at[me],
            send_sem=sum_send,
            recv_sem=sum_recv,
            device_id=(xs[a], ys[b], zs[c]),
            device_id_type=MESH,
        ).start()

    def top_copy(k):
        return pltpu.make_async_remote_copy(
            src_ref=top_own,
            dst_ref=top_in,
            send_sem=top_send.at[k],
            recv_sem=top_recv,
            device_id=(x, y, zs[k]),
            device_id_type=MESH,
        )

    @pl.when(is_top)
    def _():
        for k in range(1, nz):
            top_copy(k).start()

    for b, c in surf_offsets:

        def arrived(b=b, c=c):
            for copy in surf_copies(-b, -c):
                copy.wait_recv()

        pl.when(surf_present(b, c, True))(arrived)
    loads[3].wait()
    start = pl.multiple_of(z * share, share)
    tall = rows + 2 * STEPS
    left_half = lax.broadcasted_iota(jnp.int32, (1, width), 1) < width // 2

    def joined_window(ref):
        wide = ref[:, pl.ds(start, share + 2 * width)].astype(jnp.float32)
        rim = jnp.where(left_half, wide[:, width + share :], wide[:, :width])
        return jnp.concatenate([wide[:, width : width + share], rim], axis=1)

    work[...] = joined_window(height)
    k = joined_window(conduct)[krow - STEPS : krow + rows + STEPS]
    span = share + width
    face_right[...] = 0.5 * (k + pltpu.roll(k, span - 1, 1))
    face_down[...] = 0.5 * (k + pltpu.roll(k, tall - 1, 0))
    row_at = x * rows - STEPS + lax.broadcasted_iota(jnp.int32, (tall, span), 0)
    lane_at = lax.broadcasted_iota(jnp.int32, (tall, span), 1)
    lane_at = jnp.where(lane_at >= span - width // 2, lane_at - span, lane_at)
    col_at = y * cols + z * share + lane_at
    inside[...] = jnp.where(
        (row_at >= 0) & (row_at < rows * nx) & (col_at >= 0) & (col_at < cols * ny), time_step, 0.0
    )

    def diffuse(_, carry):
        h = work[...]
        s = pltpu.roll(h, span - 1, 1) - h
        along = face_right[...] * s * lax.rsqrt(1.0 + s * s)
        s = pltpu.roll(h, tall - 1, 0) - h
        across = face_down[...] * s * lax.rsqrt(1.0 + s * s)
        change = along - pltpu.roll(along, 1, 1) + across - pltpu.roll(across, 1, 0)
        work[...] = h + inside[...] * change
        return carry

    lax.fori_loop(0, STEPS, diffuse, 0)

    @pl.when(jnp.logical_not(is_top))
    def _():
        top_copy(1).wait_recv()
        top_own[...] = top_in[...]

    cell_at = lax.broadcasted_iota(jnp.int32, (width, share), 0) * ratio_c
    col = z * share + lax.broadcasted_iota(jnp.int32, (width, share), 1)
    pick = jnp.where((col >= cell_at) & (col < cell_at + ratio_c), 1.0, 0.0)
    spread = picked(top_own[...].reshape(2 * cells, width), pick.astype(jnp.bfloat16))

    for o in OFFSETS:
        pl.when(present(*o))(lambda o=o: rim_copy(*o).wait_send())
    for b, c in surf_offsets:

        def sent(b=b, c=c):
            for copy in surf_copies(b, c):
                copy.wait_send()

        pl.when(surf_present(b, c, False))(sent)

    @pl.when(is_top)
    def _():
        for k in range(1, nz):
            top_copy(k).wait_send()

    most = gathered.at[pl.ds(0, count - 1)]
    pltpu.make_async_copy(most, most, sum_send).wait()
    pltpu.make_async_copy(most, most, sum_recv).wait()

    table = gathered[...].reshape(count, width)
    m0, m1, own, e, ww, waw, baw = [table[:, i : i + 1] for i in range(7)]
    rr = m0.sum(axis=0, keepdims=True)
    bab = m1.sum(axis=0, keepdims=True)
    mean = bab / rr
    off = own - mean
    s2 = (ww + off * (2.0 * e + off * m0)).sum(axis=0, keepdims=True)
    q = (waw + off * (ww + own * e + baw + off * m1)).sum(axis=0, keepdims=True)
    alpha0 = rr / bab
    beta = s2 / (mean * bab)
    alpha1 = s2 / (q - s2 * s2 / bab)
    on_b = alpha0 + alpha1 * (1.0 + beta)
    on_ab = -alpha1 * alpha0
    for f in range(3):
        velocity_ref[f] = on_b * field[f] + on_ab * image[f, 1:-1, 0:cells, 0:width]
    rise = (STEPS * time_step) * (on_b * spread[:cells] + on_ab * spread[cells:])
    rise = jnp.broadcast_to(rise[:, None, :], (cells, ratio_r, share)).reshape(rows, share)
    surface_ref[...] = work[STEPS : STEPS + rows, 0:share] + rise


def put(velocity_in, surface_in, velocity_out, surface_out, sems):
    copies = [
        pltpu.make_async_copy(velocity_in, velocity_out, sems.at[0]),
        pltpu.make_async_copy(surface_in, surface_out, sems.at[1]),
    ]
    for copy in copies:
        copy.start()
    for copy in copies:
        copy.wait()


def local(sizes, body_force, viscosity, topography, kappa):
    depth, cells, width = viscosity.shape
    rows, cols = topography.shape
    nx, ny, nz = sizes
    count = nx * ny * nz
    share = cols // nz
    f32 = jnp.float32
    dma = pltpu.SemaphoreType.DMA
    made = pl.pallas_call(
        functools.partial(kernel, sizes),
        out_shape=(
            jax.ShapeDtypeStruct(body_force.shape, f32),
            jax.ShapeDtypeStruct((rows, share), f32),
        ),
        in_specs=[pl.BlockSpec(memory_space=pltpu.HBM)] * 4,
        out_specs=[pl.BlockSpec(memory_space=pltpu.VMEM)] * 2,
        scratch_shapes=[
            pltpu.VMEM((4, depth, cells, width), f32),
            pltpu.VMEM((cells, width), f32),
            pltpu.VMEM((2, depth, cells, width), f32),
            pltpu.VMEM((2, 4, REACH, cells, width), f32),
            pltpu.VMEM((2, depth, cells, width), f32),
            pltpu.VMEM((2, 2, 2, cells, width), f32),
            pltpu.VMEM((9, 2, cells, width), f32),
            pltpu.VMEM((4, depth + 2 * REACH, 2 * cells, 2 * width), f32),
            pltpu.VMEM((3, depth + 2 * REACH - 2, 2 * cells, 2 * width), f32),
            pltpu.VMEM((rows + 2 * STEPS, cols + 2 * width), f32),
            pltpu.VMEM((rows + 32, cols + 2 * width), kappa.dtype),
            pltpu.VMEM((rows + 2 * STEPS, share + width), f32),
            pltpu.VMEM((rows + 2 * STEPS, share + width), f32),
            pltpu.VMEM((rows + 2 * STEPS, share + width), f32),
            pltpu.VMEM((rows + 2 * STEPS, share + width), f32),
            pltpu.VMEM((1, 1, width), f32),
            pltpu.VMEM((count, 1, width), f32),
            pltpu.VMEM((2, cells, width), f32),
            pltpu.VMEM((2, cells, width), f32),
            dma((4,)),
            dma((27,)),
            dma((27,)),
            dma((2, 9)),
            dma((2, 9)),
            dma,
            dma,
            dma((nz,)),
            dma,
        ],
        compiler_params=pltpu.CompilerParams(
            collective_id=0, has_side_effects=True, vmem_limit_bytes=32 * 1024 * 1024
        ),
    )(*[pltpu.with_memory_space_constraint(one, pltpu.HBM) for one in (body_force, viscosity, topography, kappa)])
    return pl.pallas_call(
        put,
        out_shape=tuple(jax.ShapeDtypeStruct(one.shape, one.dtype) for one in made),
        in_specs=[pl.BlockSpec(memory_space=pltpu.VMEM)] * 2,
        out_specs=[pl.BlockSpec(memory_space=pltpu.HBM)] * 2,
        scratch_shapes=[dma((2,))],
    )(*made)


def solution(mesh):
    sizes = tuple(mesh.shape[axis] for axis in ("gx", "gy", "gz"))
    in_specs = (P(None, "gz", "gx", "gy"), P("gz", "gx", "gy"), P("gx", "gy"), P("gx", "gy"))
    out_specs = (P(None, "gz", "gx", "gy"), P("gx", ("gy", "gz")))
    return jax.shard_map(
        functools.partial(local, sizes), mesh=mesh, in_specs=in_specs, out_specs=out_specs, check_vma=False
    )
```

```python
import functools

import jax
import jax.numpy as jnp
from jax import lax
from jax.experimental import pallas as pl
from jax.experimental.pallas import tpu as pltpu
from jax.sharding import PartitionSpec as P

STEPS = 8
REACH = 2
EARLY = 4

drag = 1.0
time_step = 1.0
load_gain = 4.0

W_FACE = 0.5
W_EDGE = 0.25
W_CORNER = 0.5 / 3.0
W_ALL = 6 * W_FACE + 12 * W_EDGE + 8 * W_CORNER

MESH = pl.DeviceIdType.MESH
SIGNS = (-1, 0, 1)
OFFSETS = [(a, b, c) for a in SIGNS for b in SIGNS for c in SIGNS if (a, b, c) != (0, 0, 0)]


def side(sign):
    return 0 if sign < 0 else 1


def code(a, b, c):
    return (a + 1) * 9 + (b + 1) * 3 + (c + 1)


def weighted(u):
    rows, lanes = u.shape[1:]
    beside = pltpu.roll(u, 1, 2) + pltpu.roll(u, lanes - 1, 2)
    near = W_FACE * u + W_EDGE * beside
    far = W_EDGE * u + W_CORNER * beside
    level = W_FACE * beside[1:-1] + (near[:-2] + near[2:])
    next_row = near[1:-1] + (far[:-2] + far[2:])
    return level + (pltpu.roll(next_row, 1, 1) + pltpu.roll(next_row, rows - 1, 1))


def picked(x, choice):
    parts = []
    for _ in range(3):
        part = x.astype(jnp.bfloat16)
        parts.append(part.astype(jnp.float32))
        x = x - parts[-1]
    rows = x.shape[0]
    stacked = jnp.concatenate(parts, axis=0).astype(jnp.bfloat16)
    out = jnp.dot(stacked, choice, preferred_element_type=jnp.float32)
    return out[:rows] + (out[rows : 2 * rows] + out[2 * rows :])


def total(x):
    x = x.reshape((-1,) + x.shape[-2:]).sum(axis=0)
    return x.sum(axis=(0, 1), keepdims=True)


def kernel(
    sizes,
    force_hbm,
    visc_hbm,
    topo_hbm,
    kappa_hbm,
    velocity_ref,
    surface_ref,
    field,
    lane_pack,
    row_pack,
    from_depth,
    from_rows,
    from_rows_depth,
    from_cols,
    ext,
    image,
    height,
    conduct,
    work,
    face_right,
    face_down,
    inside,
    row_out,
    gathered,
    top_own,
    top_in,
    load_sem,
    rim_send,
    rim_recv,
    surf_send,
    surf_recv,
    sum_send,
    sum_recv,
    top_send,
    top_recv,
):
    nx, ny, nz = sizes
    count = nx * ny * nz
    x, y, z = lax.axis_index("gx"), lax.axis_index("gy"), lax.axis_index("gz")
    depth, cells, width = field.shape[1:]
    rows, cols = topo_hbm.shape
    share = cols // nz
    krow = 16

    xs = [lax.rem(x + k, nx) for k in range(nx)]
    ys = [lax.rem(y + k, ny) for k in range(ny)]
    zs = [lax.rem(z + k, nz) for k in range(nz)]
    others = [(a, b, c) for a in range(nx) for b in range(ny) for c in range(nz)][1:]
    others.sort(key=lambda o: -(min(o[0], nx - o[0]) + min(o[1], ny - o[1]) + min(o[2], nz - o[2])))
    is_top = z == nz - 1

    loads = [
        pltpu.make_async_copy(topo_hbm, height.at[STEPS : STEPS + rows, width : width + cols], load_sem.at[0]),
        pltpu.make_async_copy(force_hbm, field.at[0:3], load_sem.at[1]),
        pltpu.make_async_copy(visc_hbm, field.at[3], load_sem.at[2]),
        pltpu.make_async_copy(kappa_hbm, conduct.at[krow : krow + rows, width : width + cols], load_sem.at[3]),
    ]
    for copy in loads:
        copy.start()

    for ref in (from_depth, from_rows, from_rows_depth, from_cols):
        ref[...] = jnp.zeros_like(ref)
    height[0:STEPS, :] = jnp.zeros((STEPS, height.shape[1]), height.dtype)
    height[STEPS + rows :, :] = jnp.zeros((STEPS, height.shape[1]), height.dtype)
    height[STEPS : STEPS + rows, 0:width] = jnp.zeros((rows, width), height.dtype)
    height[STEPS : STEPS + rows, width + cols :] = jnp.zeros((rows, width), height.dtype)
    conduct[0:krow, :] = jnp.zeros((krow, conduct.shape[1]), conduct.dtype)
    conduct[krow + rows :, :] = jnp.zeros((krow, conduct.shape[1]), conduct.dtype)
    conduct[krow : krow + rows, 0:width] = jnp.zeros((rows, width), conduct.dtype)
    conduct[krow : krow + rows, width + cols :] = jnp.zeros((rows, width), conduct.dtype)

    barrier = pltpu.get_barrier_semaphore()
    for a, b, c in reversed(others):
        pl.semaphore_signal(barrier, inc=1, device_id=(xs[a], ys[b], zs[c]), device_id_type=MESH)

    ratio_r, ratio_c = rows // cells, cols // width
    at = lax.broadcasted_iota(jnp.int32, (cols, width), 0)
    first = lax.broadcasted_iota(jnp.int32, (cols, width), 1) * ratio_c
    pick = jnp.where((at >= first) & (at < first + ratio_c), 1.0, 0.0).astype(jnp.bfloat16)

    pl.semaphore_wait(barrier, count - 1)

    def present(a, b, c):
        yes = None
        for sign, at_, size in ((a, z, nz), (b, x, nx), (c, y, ny)):
            if sign:
                one = at_ > 0 if sign < 0 else at_ < size - 1
                yes = one if yes is None else jnp.logical_and(yes, one)
        return yes

    surf_offsets = [(b, c) for b in SIGNS for c in SIGNS if (b, c) != (0, 0)]

    def surf_present(b, c, receiving):
        yes = present(0, b, c)
        toward = -c if receiving else c
        if toward > 0:
            yes = jnp.logical_and(yes, z == 0)
        if toward < 0:
            yes = jnp.logical_and(yes, z == nz - 1)
        return yes

    def surf_copies(b, c):
        def spans(sign, size, halo, lead):
            if sign == 0:
                return slice(0, size), slice(lead, lead + size)
            if sign > 0:
                return slice(size - halo, size), slice(0, halo)
            return slice(0, halo), slice(lead + size, lead + size + halo)

        cs, cd = spans(c, cols, width, width)
        n = (b + 1) * 3 + (c + 1)
        m = (1 - b) * 3 + (1 - c)
        made = []
        for i, (src, dst, halo) in enumerate(((topo_hbm, height, STEPS), (kappa_hbm, conduct, krow))):
            rs, rd = spans(b, rows, halo, halo)
            made.append(
                pltpu.make_async_remote_copy(
                    src_ref=src.at[rs, cs],
                    dst_ref=dst.at[rd, cd],
                    send_sem=surf_send.at[i, n],
                    recv_sem=surf_recv.at[i, m],
                    device_id=(x + b, y + c, z),
                    device_id_type=MESH,
                )
            )
        return made

    def surf_start(b, c):
        for copy in surf_copies(b, c):
            copy.start()

    for o in surf_offsets:
        pl.when(surf_present(*o, False))(lambda o=o: surf_start(*o))

    loads[0].wait()
    by_rows = height[STEPS : STEPS + rows, width : width + cols].reshape(cells, ratio_r, cols).sum(axis=1)
    load = picked(by_rows, pick) * (1.0 / (ratio_r * ratio_c))
    loads[1].wait()
    loads[2].wait()
    field[2, depth - 1] = field[2, depth - 1] + jnp.where(is_top, -load_gain * load, 0.0)

    lane = lax.broadcasted_iota(jnp.int32, (cells, width), 1)
    sub = lax.broadcasted_iota(jnp.int32, (cells, width), 0)
    packed = jnp.zeros((cells, width), jnp.float32)
    up_pack, down_pack = {}, {}
    for f in range(4):
        for d in range(depth):
            tile = field[f, d]
            j = f * depth + d
            packed = jnp.where((lane >= 4 * j) & (lane < 4 * j + 4), pltpu.roll(tile, (4 * j + 2) % width, 1), packed)
            t, p = (d // 2) * 2 + f // 2, (d % 2) * 2 + f % 2
            chosen = (sub >= 2 * p) & (sub < 2 * p + 2)
            up = pltpu.roll(tile, (2 * p) % 8, 0) if p else tile
            down = pltpu.roll(tile, (2 * p + 2) % 8, 0) if (2 * p + 2) % 8 else tile
            up_pack[t] = jnp.where(chosen, up, up_pack.get(t, 0.0))
            down_pack[t] = jnp.where(chosen, down, down_pack.get(t, 0.0))
    lane_pack[...] = packed
    for t in range(depth):
        row_pack[0, t] = up_pack[t]
        row_pack[1, t] = down_pack[t]

    def rim_copy(a, b, c):
        span = slice(depth - 2, depth) if a > 0 else slice(0, 2)
        if c != 0:
            src, dst = lane_pack, from_cols.at[(1 - a) * 3 + (1 - b), side(-c)]
        elif b == 0:
            src, dst = field.at[:, span], from_depth.at[side(-a)]
        elif a == 0:
            src, dst = row_pack.at[side(b)], from_rows.at[side(-b)]
        else:
            src, dst = row_pack.at[side(b), span], from_rows_depth.at[side(-a), side(-b)]
        return pltpu.make_async_remote_copy(
            src_ref=src,
            dst_ref=dst,
            send_sem=rim_send.at[code(a, b, c)],
            recv_sem=rim_recv.at[code(-a, -b, -c)],
            device_id=(x + b, y + c, z + a),
            device_id_type=MESH,
        )

    for o in OFFSETS:
        pl.when(present(*o))(lambda o=o: rim_copy(*o).start())

    for b, c in surf_offsets:

        def arrived(b=b, c=c):
            for copy in surf_copies(-b, -c):
                copy.wait_recv()

        pl.when(surf_present(b, c, True))(arrived)
    loads[3].wait()
    start = pl.multiple_of(z * share, share)
    tall = rows + 2 * STEPS
    left_half = lax.broadcasted_iota(jnp.int32, (1, width), 1) < width // 2

    def joined_window(ref):
        wide = ref[:, pl.ds(start, share + 2 * width)].astype(jnp.float32)
        rim = jnp.where(left_half, wide[:, width + share :], wide[:, :width])
        return jnp.concatenate([wide[:, width : width + share], rim], axis=1)

    work[...] = joined_window(height)
    k = joined_window(conduct)[krow - STEPS : krow + rows + STEPS]
    span = share + width
    face_right[...] = 0.5 * (k + pltpu.roll(k, span - 1, 1))
    face_down[...] = 0.5 * (k + pltpu.roll(k, tall - 1, 0))
    row_at = x * rows - STEPS + lax.broadcasted_iota(jnp.int32, (tall, span), 0)
    lane_at = lax.broadcasted_iota(jnp.int32, (tall, span), 1)
    lane_at = jnp.where(lane_at >= span - width // 2, lane_at - span, lane_at)
    col_at = y * cols + z * share + lane_at
    inside[...] = jnp.where(
        (row_at >= 0) & (row_at < rows * nx) & (col_at >= 0) & (col_at < cols * ny), time_step, 0.0
    )

    def diffuse(_, carry):
        h = work[...]
        s = pltpu.roll(h, span - 1, 1) - h
        along = face_right[...] * s * lax.rsqrt(1.0 + s * s)
        s = pltpu.roll(h, tall - 1, 0) - h
        across = face_down[...] * s * lax.rsqrt(1.0 + s * s)
        change = along - pltpu.roll(along, 1, 1) + across - pltpu.roll(across, 1, 0)
        work[...] = h + inside[...] * change
        return carry

    lax.fori_loop(0, EARLY, diffuse, 0)

    for a, b, c in OFFSETS:
        pl.when(present(a, b, c))(lambda o=(-a, -b, -c): rim_copy(*o).wait_recv())
    from_low = sub < cells // 2
    from_left = (lane % 4) < 2
    for a in SIGNS:
        joined = []
        low = from_cols[(a + 1) * 3 + 1, 0]
        high = from_cols[(a + 1) * 3 + 1, 1]
        if True:
            joined.append(jnp.where(from_left, low, high))
            low = jnp.where(from_low, from_cols[(a + 1) * 3 + 2, 0], from_cols[(a + 1) * 3, 0])
            high = jnp.where(from_low, from_cols[(a + 1) * 3 + 2, 1], from_cols[(a + 1) * 3, 1])
            joined.append(jnp.where(from_left, low, high))
        for f in range(4):
            for d in range(depth) if a == 0 else (range(2) if a > 0 else range(depth - 2, depth)):
                layer = REACH + a * depth + d
                t, p = (d // 2) * 2 + f // 2, (d % 2) * 2 + f % 2
                if a == 0:
                    center, above, below = field[f, d], from_rows[0, t], from_rows[1, t]
                else:
                    center = from_depth[side(a), f, d % 2]
                    above = from_rows_depth[side(a), 0, f // 2]
                    below = from_rows_depth[side(a), 1, f // 2]
                above = pltpu.roll(above, 6 - 2 * p, 0) if p != 3 else above
                below = pltpu.roll(below, 8 - 2 * p, 0) if p else below
                j = f * depth + d
                ext[f, layer, 0:cells, 0:width] = center
                ext[f, layer, cells:, 0:width] = jnp.where(from_low, below, above)
                turn = (width - 2 - 4 * j) % width
                for r in range(2):
                    tile = pltpu.roll(joined[r], turn, 1) if turn else joined[r]
                    ext[f, layer, r * cells : (r + 1) * cells, width:] = tile

    eta = ext[3]
    gain = drag + W_ALL * eta[1:-1] + weighted(eta)
    for f in range(3):
        v = ext[f]
        out = gain * v[1:-1] - eta[1:-1] * weighted(v) - weighted(eta * v)
        image[f] = jnp.where(eta[1:-1] > 0.0, out, 0.0)
    eta1 = eta[1:-1]
    center = (slice(None), slice(0, cells), slice(0, width))
    m0 = m1 = jnp.zeros((cells, width), jnp.float32)
    for f in range(3):
        b = field[f]
        ab = image[f, 1:-1, 0:cells, 0:width]
        m0 = m0 + (b * b).sum(axis=0)
        m1 = m1 + (b * ab).sum(axis=0)
    m0, m1 = total(m0), total(m1)
    own = jnp.where(m0 > 0.0, m1 / m0, 0.0)
    sums = [jnp.zeros((cells, width), jnp.float32) for _ in range(4)]
    for f in range(3):
        v = image[f]
        b = field[f]
        ab = v[1:-1][center]
        again = (
            gain[1:-1][center] * ab
            - eta1[1:-1][center] * weighted(v)[center]
            - weighted(eta1 * v)[center]
        )
        w = ab - own * b
        aw = again - own * ab
        for i, (p, q) in enumerate(((w, b), (w, w), (w, aw), (b, aw))):
            sums[i] = sums[i] + (p * q).sum(axis=0)
    numbers = [m0, m1, own] + [total(s) for s in sums]
    spot = lax.broadcasted_iota(jnp.int32, (1, width), 1)
    line = jnp.zeros((1, width), jnp.float32)
    for i, number in enumerate(numbers):
        line = jnp.where(spot == i, number, line)
    row_out[0] = line
    me = (x * ny + y) * nz + z
    gathered[me] = line
    top_own[0] = field[2, depth - 1]
    top_own[1] = image[2, depth, 0:cells, 0:width]
    for a, b, c in others:
        pltpu.make_async_remote_copy(
            src_ref=row_out.at[0],
            dst_ref=gathered.at[me],
            send_sem=sum_send,
            recv_sem=sum_recv,
            device_id=(xs[a], ys[b], zs[c]),
            device_id_type=MESH,
        ).start()

    def top_copy(k):
        return pltpu.make_async_remote_copy(
            src_ref=top_own,
            dst_ref=top_in,
            send_sem=top_send.at[k],
            recv_sem=top_recv,
            device_id=(x, y, zs[k]),
            device_id_type=MESH,
        )

    @pl.when(is_top)
    def _():
        for k in range(1, nz):
            top_copy(k).start()

    lax.fori_loop(EARLY, STEPS, diffuse, 0)

    @pl.when(jnp.logical_not(is_top))
    def _():
        top_copy(1).wait_recv()
        top_own[...] = top_in[...]

    cell_at = lax.broadcasted_iota(jnp.int32, (width, share), 0) * ratio_c
    col = z * share + lax.broadcasted_iota(jnp.int32, (width, share), 1)
    pick = jnp.where((col >= cell_at) & (col < cell_at + ratio_c), 1.0, 0.0)
    spread = picked(top_own[...].reshape(2 * cells, width), pick.astype(jnp.bfloat16))

    for o in OFFSETS:
        pl.when(present(*o))(lambda o=o: rim_copy(*o).wait_send())
    for b, c in surf_offsets:

        def sent(b=b, c=c):
            for copy in surf_copies(b, c):
                copy.wait_send()

        pl.when(surf_present(b, c, False))(sent)

    @pl.when(is_top)
    def _():
        for k in range(1, nz):
            top_copy(k).wait_send()

    most = gathered.at[pl.ds(0, count - 1)]
    pltpu.make_async_copy(most, most, sum_send).wait()
    pltpu.make_async_copy(most, most, sum_recv).wait()

    table = gathered[...].reshape(count, width)
    m0, m1, own, e, ww, waw, baw = [table[:, i : i + 1] for i in range(7)]
    rr = m0.sum(axis=0, keepdims=True)
    bab = m1.sum(axis=0, keepdims=True)
    mean = bab / rr
    off = own - mean
    s2 = (ww + off * (2.0 * e + off * m0)).sum(axis=0, keepdims=True)
    q = (waw + off * (ww + own * e + baw + off * m1)).sum(axis=0, keepdims=True)
    alpha0 = rr / bab
    beta = s2 / (mean * bab)
    alpha1 = s2 / (q - s2 * s2 / bab)
    on_b = alpha0 + alpha1 * (1.0 + beta)
    on_ab = -alpha1 * alpha0
    for f in range(3):
        velocity_ref[f] = on_b * field[f] + on_ab * image[f, 1:-1, 0:cells, 0:width]
    rise = (STEPS * time_step) * (on_b * spread[:cells] + on_ab * spread[cells:])
    rise = jnp.broadcast_to(rise[:, None, :], (cells, ratio_r, share)).reshape(rows, share)
    surface_ref[...] = work[STEPS : STEPS + rows, 0:share] + rise


def local(sizes, body_force, viscosity, topography, kappa):
    depth, cells, width = viscosity.shape
    rows, cols = topography.shape
    nx, ny, nz = sizes
    count = nx * ny * nz
    share = cols // nz
    f32 = jnp.float32
    dma = pltpu.SemaphoreType.DMA
    return pl.pallas_call(
        functools.partial(kernel, sizes),
        out_shape=(
            jax.ShapeDtypeStruct(body_force.shape, f32),
            jax.ShapeDtypeStruct((rows, share), f32),
        ),
        in_specs=[pl.BlockSpec(memory_space=pltpu.HBM)] * 4,
        out_specs=[pl.BlockSpec(memory_space=pltpu.VMEM)] * 2,
        scratch_shapes=[
            pltpu.VMEM((4, depth, cells, width), f32),
            pltpu.VMEM((cells, width), f32),
            pltpu.VMEM((2, depth, cells, width), f32),
            pltpu.VMEM((2, 4, REACH, cells, width), f32),
            pltpu.VMEM((2, depth, cells, width), f32),
            pltpu.VMEM((2, 2, 2, cells, width), f32),
            pltpu.VMEM((9, 2, cells, width), f32),
            pltpu.VMEM((4, depth + 2 * REACH, 2 * cells, 2 * width), f32),
            pltpu.VMEM((3, depth + 2 * REACH - 2, 2 * cells, 2 * width), f32),
            pltpu.VMEM((rows + 2 * STEPS, cols + 2 * width), f32),
            pltpu.VMEM((rows + 32, cols + 2 * width), kappa.dtype),
            pltpu.VMEM((rows + 2 * STEPS, share + width), f32),
            pltpu.VMEM((rows + 2 * STEPS, share + width), f32),
            pltpu.VMEM((rows + 2 * STEPS, share + width), f32),
            pltpu.VMEM((rows + 2 * STEPS, share + width), f32),
            pltpu.VMEM((1, 1, width), f32),
            pltpu.VMEM((count, 1, width), f32),
            pltpu.VMEM((2, cells, width), f32),
            pltpu.VMEM((2, cells, width), f32),
            dma((4,)),
            dma((27,)),
            dma((27,)),
            dma((2, 9)),
            dma((2, 9)),
            dma,
            dma,
            dma((nz,)),
            dma,
        ],
        compiler_params=pltpu.CompilerParams(
            collective_id=0, has_side_effects=True, vmem_limit_bytes=32 * 1024 * 1024
        ),
    )(*[pltpu.with_memory_space_constraint(one, pltpu.HBM) for one in (body_force, viscosity, topography, kappa)])


def solution(mesh):
    sizes = tuple(mesh.shape[axis] for axis in ("gx", "gy", "gz"))
    in_specs = (P(None, "gz", "gx", "gy"), P("gz", "gx", "gy"), P("gx", "gy"), P("gx", "gy"))
    out_specs = (P(None, "gz", "gx", "gy"), P("gx", ("gy", "gz")))
    return jax.shard_map(
        functools.partial(local, sizes), mesh=mesh, in_specs=in_specs, out_specs=out_specs, check_vma=False
    )
```

```python
import functools

import jax
import jax.numpy as jnp
from jax import lax
from jax.experimental import pallas as pl
from jax.experimental.pallas import tpu as pltpu
from jax.sharding import PartitionSpec as P

STEPS = 8
REACH = 2

drag = 1.0
time_step = 1.0
load_gain = 4.0

W_FACE = 0.5
W_EDGE = 0.25
W_CORNER = 0.5 / 3.0
W_ALL = 6 * W_FACE + 12 * W_EDGE + 8 * W_CORNER

MESH = pl.DeviceIdType.MESH
SIGNS = (-1, 0, 1)
OFFSETS = [(a, b, c) for a in SIGNS for b in SIGNS for c in SIGNS if (a, b, c) != (0, 0, 0)]


def side(sign):
    return 0 if sign < 0 else 1


def code(a, b, c):
    return (a + 1) * 9 + (b + 1) * 3 + (c + 1)


def weighted(u):
    rows, lanes = u.shape[1:]
    beside = pltpu.roll(u, 1, 2) + pltpu.roll(u, lanes - 1, 2)
    near = W_FACE * u + W_EDGE * beside
    far = W_EDGE * u + W_CORNER * beside
    level = W_FACE * beside[1:-1] + (near[:-2] + near[2:])
    next_row = near[1:-1] + (far[:-2] + far[2:])
    return level + (pltpu.roll(next_row, 1, 1) + pltpu.roll(next_row, rows - 1, 1))


def picked(x, choice):
    parts = []
    for _ in range(3):
        part = x.astype(jnp.bfloat16)
        parts.append(part.astype(jnp.float32))
        x = x - parts[-1]
    rows = x.shape[0]
    stacked = jnp.concatenate(parts, axis=0).astype(jnp.bfloat16)
    out = jnp.dot(stacked, choice, preferred_element_type=jnp.float32)
    return out[:rows] + (out[rows : 2 * rows] + out[2 * rows :])


def total(x):
    x = x.reshape((-1,) + x.shape[-2:]).sum(axis=0)
    return x.sum(axis=(0, 1), keepdims=True)


def kernel(
    sizes,
    force_hbm,
    visc_hbm,
    topo_hbm,
    kappa_hbm,
    velocity_ref,
    surface_ref,
    field,
    lane_pack,
    row_pack,
    from_depth,
    from_rows,
    from_rows_depth,
    from_cols,
    ext,
    image,
    height,
    conduct,
    work,
    face_right,
    face_down,
    inside,
    row_out,
    gathered,
    top_own,
    top_in,
    load_sem,
    rim_send,
    rim_recv,
    surf_send,
    surf_recv,
    sum_send,
    sum_recv,
    top_send,
    top_recv,
):
    nx, ny, nz = sizes
    count = nx * ny * nz
    x, y, z = lax.axis_index("gx"), lax.axis_index("gy"), lax.axis_index("gz")
    depth, cells, width = field.shape[1:]
    rows, cols = topo_hbm.shape
    share = cols // nz
    krow = 16

    xs = [lax.rem(x + k, nx) for k in range(nx)]
    ys = [lax.rem(y + k, ny) for k in range(ny)]
    zs = [lax.rem(z + k, nz) for k in range(nz)]
    others = [(a, b, c) for a in range(nx) for b in range(ny) for c in range(nz)][1:]
    others.sort(key=lambda o: -(min(o[0], nx - o[0]) + min(o[1], ny - o[1]) + min(o[2], nz - o[2])))
    is_top = z == nz - 1

    loads = [
        pltpu.make_async_copy(topo_hbm, height.at[STEPS : STEPS + rows, width : width + cols], load_sem.at[0]),
        pltpu.make_async_copy(force_hbm, field.at[0:3], load_sem.at[1]),
        pltpu.make_async_copy(visc_hbm, field.at[3], load_sem.at[2]),
        pltpu.make_async_copy(kappa_hbm, conduct.at[krow : krow + rows, width : width + cols], load_sem.at[3]),
    ]
    for copy in loads:
        copy.start()

    for ref in (from_depth, from_rows, from_rows_depth, from_cols):
        ref[...] = jnp.zeros_like(ref)
    height[0:STEPS, :] = jnp.zeros((STEPS, height.shape[1]), height.dtype)
    height[STEPS + rows :, :] = jnp.zeros((STEPS, height.shape[1]), height.dtype)
    height[STEPS : STEPS + rows, 0:width] = jnp.zeros((rows, width), height.dtype)
    height[STEPS : STEPS + rows, width + cols :] = jnp.zeros((rows, width), height.dtype)
    conduct[0:krow, :] = jnp.zeros((krow, conduct.shape[1]), conduct.dtype)
    conduct[krow + rows :, :] = jnp.zeros((krow, conduct.shape[1]), conduct.dtype)
    conduct[krow : krow + rows, 0:width] = jnp.zeros((rows, width), conduct.dtype)
    conduct[krow : krow + rows, width + cols :] = jnp.zeros((rows, width), conduct.dtype)

    barrier = pltpu.get_barrier_semaphore()
    for a, b, c in reversed(others):
        pl.semaphore_signal(barrier, inc=1, device_id=(xs[a], ys[b], zs[c]), device_id_type=MESH)

    ratio_r, ratio_c = rows // cells, cols // width
    at = lax.broadcasted_iota(jnp.int32, (cols, width), 0)
    first = lax.broadcasted_iota(jnp.int32, (cols, width), 1) * ratio_c
    pick = jnp.where((at >= first) & (at < first + ratio_c), 1.0, 0.0).astype(jnp.bfloat16)

    def present(a, b, c):
        yes = None
        for sign, at_, size in ((a, z, nz), (b, x, nx), (c, y, ny)):
            if sign:
                one = at_ > 0 if sign < 0 else at_ < size - 1
                yes = one if yes is None else jnp.logical_and(yes, one)
        return yes

    loads[0].wait()
    by_rows = height[STEPS : STEPS + rows, width : width + cols].reshape(cells, ratio_r, cols).sum(axis=1)
    load = picked(by_rows, pick) * (1.0 / (ratio_r * ratio_c))
    loads[1].wait()
    loads[2].wait()
    field[2, depth - 1] = field[2, depth - 1] + jnp.where(is_top, -load_gain * load, 0.0)

    lane = lax.broadcasted_iota(jnp.int32, (cells, width), 1)
    sub = lax.broadcasted_iota(jnp.int32, (cells, width), 0)
    packed = jnp.zeros((cells, width), jnp.float32)
    up_pack, down_pack = {}, {}
    for f in range(4):
        for d in range(depth):
            tile = field[f, d]
            j = f * depth + d
            packed = jnp.where((lane >= 4 * j) & (lane < 4 * j + 4), pltpu.roll(tile, (4 * j + 2) % width, 1), packed)
            t, p = (d // 2) * 2 + f // 2, (d % 2) * 2 + f % 2
            chosen = (sub >= 2 * p) & (sub < 2 * p + 2)
            up = pltpu.roll(tile, (2 * p) % 8, 0) if p else tile
            down = pltpu.roll(tile, (2 * p + 2) % 8, 0) if (2 * p + 2) % 8 else tile
            up_pack[t] = jnp.where(chosen, up, up_pack.get(t, 0.0))
            down_pack[t] = jnp.where(chosen, down, down_pack.get(t, 0.0))
    lane_pack[...] = packed
    for t in range(depth):
        row_pack[0, t] = up_pack[t]
        row_pack[1, t] = down_pack[t]

    def rim_copy(a, b, c):
        span = slice(depth - 2, depth) if a > 0 else slice(0, 2)
        if c != 0:
            src, dst = lane_pack, from_cols.at[(1 - a) * 3 + (1 - b), side(-c)]
        elif b == 0:
            src, dst = field.at[:, span], from_depth.at[side(-a)]
        elif a == 0:
            src, dst = row_pack.at[side(b)], from_rows.at[side(-b)]
        else:
            src, dst = row_pack.at[side(b), span], from_rows_depth.at[side(-a), side(-b)]
        return pltpu.make_async_remote_copy(
            src_ref=src,
            dst_ref=dst,
            send_sem=rim_send.at[code(a, b, c)],
            recv_sem=rim_recv.at[code(-a, -b, -c)],
            device_id=(x + b, y + c, z + a),
            device_id_type=MESH,
        )

    pl.semaphore_wait(barrier, count - 1)
    for o in OFFSETS:
        pl.when(present(*o))(lambda o=o: rim_copy(*o).start())

    surf_offsets = [(b, c) for b in SIGNS for c in SIGNS if (b, c) != (0, 0)]

    def surf_present(b, c, receiving):
        yes = present(0, b, c)
        toward = -c if receiving else c
        if toward > 0:
            yes = jnp.logical_and(yes, z == 0)
        if toward < 0:
            yes = jnp.logical_and(yes, z == nz - 1)
        return yes

    def surf_copies(b, c):
        def spans(sign, size, halo, lead):
            if sign == 0:
                return slice(0, size), slice(lead, lead + size)
            if sign > 0:
                return slice(size - halo, size), slice(0, halo)
            return slice(0, halo), slice(lead + size, lead + size + halo)

        cs, cd = spans(c, cols, width, width)
        n = (b + 1) * 3 + (c + 1)
        m = (1 - b) * 3 + (1 - c)
        made = []
        for i, (src, dst, halo) in enumerate(((topo_hbm, height, STEPS), (kappa_hbm, conduct, krow))):
            rs, rd = spans(b, rows, halo, halo)
            made.append(
                pltpu.make_async_remote_copy(
                    src_ref=src.at[rs, cs],
                    dst_ref=dst.at[rd, cd],
                    send_sem=surf_send.at[i, n],
                    recv_sem=surf_recv.at[i, m],
                    device_id=(x + b, y + c, z),
                    device_id_type=MESH,
                )
            )
        return made

    def surf_start(b, c):
        for copy in surf_copies(b, c):
            copy.start()

    for o in surf_offsets:
        pl.when(surf_present(*o, False))(lambda o=o: surf_start(*o))

    for a, b, c in OFFSETS:
        pl.when(present(a, b, c))(lambda o=(-a, -b, -c): rim_copy(*o).wait_recv())
    from_low = sub < cells // 2
    from_left = (lane % 4) < 2
    for a in SIGNS:
        joined = []
        low = from_cols[(a + 1) * 3 + 1, 0]
        high = from_cols[(a + 1) * 3 + 1, 1]
        if True:
            joined.append(jnp.where(from_left, low, high))
            low = jnp.where(from_low, from_cols[(a + 1) * 3 + 2, 0], from_cols[(a + 1) * 3, 0])
            high = jnp.where(from_low, from_cols[(a + 1) * 3 + 2, 1], from_cols[(a + 1) * 3, 1])
            joined.append(jnp.where(from_left, low, high))
        for f in range(4):
            for d in range(depth) if a == 0 else (range(2) if a > 0 else range(depth - 2, depth)):
                layer = REACH + a * depth + d
                t, p = (d // 2) * 2 + f // 2, (d % 2) * 2 + f % 2
                if a == 0:
                    center, above, below = field[f, d], from_rows[0, t], from_rows[1, t]
                else:
                    center = from_depth[side(a), f, d % 2]
                    above = from_rows_depth[side(a), 0, f // 2]
                    below = from_rows_depth[side(a), 1, f // 2]
                above = pltpu.roll(above, 6 - 2 * p, 0) if p != 3 else above
                below = pltpu.roll(below, 8 - 2 * p, 0) if p else below
                j = f * depth + d
                ext[f, layer, 0:cells, 0:width] = center
                ext[f, layer, cells:, 0:width] = jnp.where(from_low, below, above)
                turn = (width - 2 - 4 * j) % width
                for r in range(2):
                    tile = pltpu.roll(joined[r], turn, 1) if turn else joined[r]
                    ext[f, layer, r * cells : (r + 1) * cells, width:] = tile

    eta = ext[3]
    gain = drag + W_ALL * eta[1:-1] + weighted(eta)
    for f in range(3):
        v = ext[f]
        out = gain * v[1:-1] - eta[1:-1] * weighted(v) - weighted(eta * v)
        image[f] = jnp.where(eta[1:-1] > 0.0, out, 0.0)
    eta1 = eta[1:-1]
    center = (slice(None), slice(0, cells), slice(0, width))
    m0 = m1 = jnp.zeros((cells, width), jnp.float32)
    for f in range(3):
        b = field[f]
        ab = image[f, 1:-1, 0:cells, 0:width]
        m0 = m0 + (b * b).sum(axis=0)
        m1 = m1 + (b * ab).sum(axis=0)
    m0, m1 = total(m0), total(m1)
    own = jnp.where(m0 > 0.0, m1 / m0, 0.0)
    sums = [jnp.zeros((cells, width), jnp.float32) for _ in range(4)]
    for f in range(3):
        v = image[f]
        b = field[f]
        ab = v[1:-1][center]
        again = (
            gain[1:-1][center] * ab
            - eta1[1:-1][center] * weighted(v)[center]
            - weighted(eta1 * v)[center]
        )
        w = ab - own * b
        aw = again - own * ab
        for i, (p, q) in enumerate(((w, b), (w, w), (w, aw), (b, aw))):
            sums[i] = sums[i] + (p * q).sum(axis=0)
    numbers = [m0, m1, own] + [total(s) for s in sums]
    spot = lax.broadcasted_iota(jnp.int32, (1, width), 1)
    line = jnp.zeros((1, width), jnp.float32)
    for i, number in enumerate(numbers):
        line = jnp.where(spot == i, number, line)
    row_out[0] = line
    me = (x * ny + y) * nz + z
    gathered[me] = line
    top_own[0] = field[2, depth - 1]
    top_own[1] = image[2, depth, 0:cells, 0:width]
    for a, b, c in others:
        pltpu.make_async_remote_copy(
            src_ref=row_out.at[0],
            dst_ref=gathered.at[me],
            send_sem=sum_send,
            recv_sem=sum_recv,
            device_id=(xs[a], ys[b], zs[c]),
            device_id_type=MESH,
        ).start()

    def top_copy(k):
        return pltpu.make_async_remote_copy(
            src_ref=top_own,
            dst_ref=top_in,
            send_sem=top_send.at[k],
            recv_sem=top_recv,
            device_id=(x, y, zs[k]),
            device_id_type=MESH,
        )

    @pl.when(is_top)
    def _():
        for k in range(1, nz):
            top_copy(k).start()

    for b, c in surf_offsets:

        def arrived(b=b, c=c):
            for copy in surf_copies(-b, -c):
                copy.wait_recv()

        pl.when(surf_present(b, c, True))(arrived)
    loads[3].wait()
    start = pl.multiple_of(z * share, share)
    tall = rows + 2 * STEPS
    left_half = lax.broadcasted_iota(jnp.int32, (1, width), 1) < width // 2

    def joined_window(ref):
        wide = ref[:, pl.ds(start, share + 2 * width)].astype(jnp.float32)
        rim = jnp.where(left_half, wide[:, width + share :], wide[:, :width])
        return jnp.concatenate([wide[:, width : width + share], rim], axis=1)

    work[...] = joined_window(height)
    k = joined_window(conduct)[krow - STEPS : krow + rows + STEPS]
    span = share + width
    face_right[...] = 0.5 * (k + pltpu.roll(k, span - 1, 1))
    face_down[...] = 0.5 * (k + pltpu.roll(k, tall - 1, 0))
    row_at = x * rows - STEPS + lax.broadcasted_iota(jnp.int32, (tall, span), 0)
    lane_at = lax.broadcasted_iota(jnp.int32, (tall, span), 1)
    lane_at = jnp.where(lane_at >= span - width // 2, lane_at - span, lane_at)
    col_at = y * cols + z * share + lane_at
    inside[...] = jnp.where(
        (row_at >= 0) & (row_at < rows * nx) & (col_at >= 0) & (col_at < cols * ny), time_step, 0.0
    )

    def diffuse(_, carry):
        h = work[...]
        s = pltpu.roll(h, span - 1, 1) - h
        along = face_right[...] * s * lax.rsqrt(1.0 + s * s)
        s = pltpu.roll(h, tall - 1, 0) - h
        across = face_down[...] * s * lax.rsqrt(1.0 + s * s)
        change = along - pltpu.roll(along, 1, 1) + across - pltpu.roll(across, 1, 0)
        work[...] = h + inside[...] * change
        return carry

    lax.fori_loop(0, STEPS, diffuse, 0)

    @pl.when(jnp.logical_not(is_top))
    def _():
        top_copy(1).wait_recv()
        top_own[...] = top_in[...]

    cell_at = lax.broadcasted_iota(jnp.int32, (width, share), 0) * ratio_c
    col = z * share + lax.broadcasted_iota(jnp.int32, (width, share), 1)
    pick = jnp.where((col >= cell_at) & (col < cell_at + ratio_c), 1.0, 0.0)
    spread = picked(top_own[...].reshape(2 * cells, width), pick.astype(jnp.bfloat16))

    for o in OFFSETS:
        pl.when(present(*o))(lambda o=o: rim_copy(*o).wait_send())
    for b, c in surf_offsets:

        def sent(b=b, c=c):
            for copy in surf_copies(b, c):
                copy.wait_send()

        pl.when(surf_present(b, c, False))(sent)

    @pl.when(is_top)
    def _():
        for k in range(1, nz):
            top_copy(k).wait_send()

    most = gathered.at[pl.ds(0, count - 1)]
    pltpu.make_async_copy(most, most, sum_send).wait()
    pltpu.make_async_copy(most, most, sum_recv).wait()

    table = gathered[...].reshape(count, width)
    m0, m1, own, e, ww, waw, baw = [table[:, i : i + 1] for i in range(7)]
    rr = m0.sum(axis=0, keepdims=True)
    bab = m1.sum(axis=0, keepdims=True)
    mean = bab / rr
    off = own - mean
    s2 = (ww + off * (2.0 * e + off * m0)).sum(axis=0, keepdims=True)
    q = (waw + off * (ww + own * e + baw + off * m1)).sum(axis=0, keepdims=True)
    alpha0 = rr / bab
    beta = s2 / (mean * bab)
    alpha1 = s2 / (q - s2 * s2 / bab)
    on_b = alpha0 + alpha1 * (1.0 + beta)
    on_ab = -alpha1 * alpha0
    for f in range(3):
        velocity_ref[f] = on_b * field[f] + on_ab * image[f, 1:-1, 0:cells, 0:width]
    rise = (STEPS * time_step) * (on_b * spread[:cells] + on_ab * spread[cells:])
    rise = jnp.broadcast_to(rise[:, None, :], (cells, ratio_r, share)).reshape(rows, share)
    surface_ref[...] = work[STEPS : STEPS + rows, 0:share] + rise


def local(sizes, body_force, viscosity, topography, kappa):
    depth, cells, width = viscosity.shape
    rows, cols = topography.shape
    nx, ny, nz = sizes
    count = nx * ny * nz
    share = cols // nz
    f32 = jnp.float32
    dma = pltpu.SemaphoreType.DMA
    return pl.pallas_call(
        functools.partial(kernel, sizes),
        out_shape=(
            jax.ShapeDtypeStruct(body_force.shape, f32),
            jax.ShapeDtypeStruct((rows, share), f32),
        ),
        in_specs=[pl.BlockSpec(memory_space=pltpu.HBM)] * 4,
        out_specs=[pl.BlockSpec(memory_space=pltpu.VMEM)] * 2,
        scratch_shapes=[
            pltpu.VMEM((4, depth, cells, width), f32),
            pltpu.VMEM((cells, width), f32),
            pltpu.VMEM((2, depth, cells, width), f32),
            pltpu.VMEM((2, 4, REACH, cells, width), f32),
            pltpu.VMEM((2, depth, cells, width), f32),
            pltpu.VMEM((2, 2, 2, cells, width), f32),
            pltpu.VMEM((9, 2, cells, width), f32),
            pltpu.VMEM((4, depth + 2 * REACH, 2 * cells, 2 * width), f32),
            pltpu.VMEM((3, depth + 2 * REACH - 2, 2 * cells, 2 * width), f32),
            pltpu.VMEM((rows + 2 * STEPS, cols + 2 * width), f32),
            pltpu.VMEM((rows + 32, cols + 2 * width), kappa.dtype),
            pltpu.VMEM((rows + 2 * STEPS, share + width), f32),
            pltpu.VMEM((rows + 2 * STEPS, share + width), f32),
            pltpu.VMEM((rows + 2 * STEPS, share + width), f32),
            pltpu.VMEM((rows + 2 * STEPS, share + width), f32),
            pltpu.VMEM((1, 1, width), f32),
            pltpu.VMEM((count, 1, width), f32),
            pltpu.VMEM((2, cells, width), f32),
            pltpu.VMEM((2, cells, width), f32),
            dma((4,)),
            dma((27,)),
            dma((27,)),
            dma((2, 9)),
            dma((2, 9)),
            dma,
            dma,
            dma((nz,)),
            dma,
        ],
        compiler_params=pltpu.CompilerParams(
            collective_id=0, has_side_effects=True, vmem_limit_bytes=32 * 1024 * 1024
        ),
    )(*[pltpu.with_memory_space_constraint(one, pltpu.HBM) for one in (body_force, viscosity, topography, kappa)])


def solution(mesh):
    sizes = tuple(mesh.shape[axis] for axis in ("gx", "gy", "gz"))
    in_specs = (P(None, "gz", "gx", "gy"), P("gz", "gx", "gy"), P("gx", "gy"), P("gx", "gy"))
    out_specs = (P(None, "gz", "gx", "gy"), P("gx", ("gy", "gz")))
    return jax.shard_map(
        functools.partial(local, sizes), mesh=mesh, in_specs=in_specs, out_specs=out_specs, check_vma=False
    )
```

```python
import functools

import jax
import jax.numpy as jnp
from jax import lax
from jax.experimental import pallas as pl
from jax.experimental.pallas import tpu as pltpu
from jax.sharding import PartitionSpec as P

STEPS = 8
REACH = 2
EARLY = 3

drag = 1.0
time_step = 1.0
load_gain = 4.0

W_FACE = 0.5
W_EDGE = 0.25
W_CORNER = 0.5 / 3.0
W_ALL = 6 * W_FACE + 12 * W_EDGE + 8 * W_CORNER

MESH = pl.DeviceIdType.MESH
SIGNS = (-1, 0, 1)
OFFSETS = sorted(
    [(a, b, c) for a in SIGNS for b in SIGNS for c in SIGNS if (a, b, c) != (0, 0, 0)],
    key=lambda o: (abs(o[0]) + abs(o[1]) + abs(o[2]), abs(o[2])),
)


def side(sign):
    return 0 if sign < 0 else 1


def code(a, b, c):
    return (a + 1) * 9 + (b + 1) * 3 + (c + 1)


def weighted(u):
    rows, lanes = u.shape[1:]
    beside = pltpu.roll(u, 1, 2) + pltpu.roll(u, lanes - 1, 2)
    near = W_FACE * u + W_EDGE * beside
    far = W_EDGE * u + W_CORNER * beside
    level = W_FACE * beside[1:-1] + (near[:-2] + near[2:])
    next_row = near[1:-1] + (far[:-2] + far[2:])
    return level + (pltpu.roll(next_row, 1, 1) + pltpu.roll(next_row, rows - 1, 1))


def picked(x, choice):
    parts = []
    for _ in range(3):
        part = x.astype(jnp.bfloat16)
        parts.append(part.astype(jnp.float32))
        x = x - parts[-1]
    rows = x.shape[0]
    stacked = jnp.concatenate(parts, axis=0).astype(jnp.bfloat16)
    out = jnp.dot(stacked, choice, preferred_element_type=jnp.float32)
    return out[:rows] + (out[rows : 2 * rows] + out[2 * rows :])


def total(x):
    x = x.reshape((-1,) + x.shape[-2:]).sum(axis=0)
    return x.sum(axis=(0, 1), keepdims=True)


def kernel(
    sizes,
    force_hbm,
    visc_hbm,
    topo_hbm,
    kappa_hbm,
    velocity_ref,
    surface_ref,
    field,
    lane_pack,
    row_pack,
    from_depth,
    from_rows,
    from_rows_depth,
    from_cols,
    ext,
    image,
    height,
    conduct,
    work,
    face_right,
    face_down,
    inside,
    row_out,
    gathered,
    top_own,
    top_in,
    load_sem,
    rim_send,
    rim_recv,
    surf_send,
    surf_recv,
    sum_send,
    sum_recv,
    top_send,
    top_recv,
):
    nx, ny, nz = sizes
    count = nx * ny * nz
    x, y, z = lax.axis_index("gx"), lax.axis_index("gy"), lax.axis_index("gz")
    depth, cells, width = field.shape[1:]
    rows, cols = topo_hbm.shape
    share = cols // nz
    krow = 16

    xs = [lax.rem(x + k, nx) for k in range(nx)]
    ys = [lax.rem(y + k, ny) for k in range(ny)]
    zs = [lax.rem(z + k, nz) for k in range(nz)]
    is_top = z == nz - 1

    loads = [
        pltpu.make_async_copy(topo_hbm, height.at[STEPS : STEPS + rows, width : width + cols], load_sem.at[0]),
        pltpu.make_async_copy(force_hbm, field.at[0:3], load_sem.at[1]),
        pltpu.make_async_copy(visc_hbm, field.at[3], load_sem.at[2]),
        pltpu.make_async_copy(kappa_hbm, conduct.at[krow : krow + rows, width : width + cols], load_sem.at[3]),
    ]
    for copy in loads:
        copy.start()

    for ref in (from_depth, from_rows, from_rows_depth, from_cols):
        ref[...] = jnp.zeros_like(ref)
    height[0:STEPS, :] = jnp.zeros((STEPS, height.shape[1]), height.dtype)
    height[STEPS + rows :, :] = jnp.zeros((STEPS, height.shape[1]), height.dtype)
    height[STEPS : STEPS + rows, 0:width] = jnp.zeros((rows, width), height.dtype)
    height[STEPS : STEPS + rows, width + cols :] = jnp.zeros((rows, width), height.dtype)
    conduct[0:krow, :] = jnp.zeros((krow, conduct.shape[1]), conduct.dtype)
    conduct[krow + rows :, :] = jnp.zeros((krow, conduct.shape[1]), conduct.dtype)
    conduct[krow : krow + rows, 0:width] = jnp.zeros((rows, width), conduct.dtype)
    conduct[krow : krow + rows, width + cols :] = jnp.zeros((rows, width), conduct.dtype)

    barrier = pltpu.get_barrier_semaphore()
    plane = nx * nz
    in_plane = [(a, c) for a in range(nx) for c in range(nz)]

    def greet(a, at_y, c):
        pl.semaphore_signal(barrier, inc=1, device_id=(xs[a], at_y, zs[c]), device_id_type=MESH)

    def greet_plane(at_y):
        for a, c in in_plane:
            greet(a, at_y, c)

    for a, c in in_plane[1:]:
        greet(a, y, c)
    pl.when(y > 0)(lambda: greet_plane(y - 1))
    pl.when(y < ny - 1)(lambda: greet_plane(y + 1))
    for k in range(ny):
        pl.when(jnp.logical_or(y - k > 1, k - y > 1))(lambda k=k: greet(0, k, 0))
    beside_y = jnp.where(y > 0, 1, 0) + jnp.where(y < ny - 1, 1, 0)
    greeted = plane + ny - 2 + (plane - 1) * beside_y

    ratio_r, ratio_c = rows // cells, cols // width
    at = lax.broadcasted_iota(jnp.int32, (cols, width), 0)
    first = lax.broadcasted_iota(jnp.int32, (cols, width), 1) * ratio_c
    pick = jnp.where((at >= first) & (at < first + ratio_c), 1.0, 0.0).astype(jnp.bfloat16)

    def present(a, b, c):
        yes = None
        for sign, at_, size in ((a, z, nz), (b, x, nx), (c, y, ny)):
            if sign:
                one = at_ > 0 if sign < 0 else at_ < size - 1
                yes = one if yes is None else jnp.logical_and(yes, one)
        return yes

    loads[0].wait()
    by_rows = height[STEPS : STEPS + rows, width : width + cols].reshape(cells, ratio_r, cols).sum(axis=1)
    load = picked(by_rows, pick) * (1.0 / (ratio_r * ratio_c))
    loads[1].wait()
    loads[2].wait()
    field[2, depth - 1] = field[2, depth - 1] + jnp.where(is_top, -load_gain * load, 0.0)

    lane = lax.broadcasted_iota(jnp.int32, (cells, width), 1)
    sub = lax.broadcasted_iota(jnp.int32, (cells, width), 0)
    packed = jnp.zeros((cells, width), jnp.float32)
    up_pack, down_pack = {}, {}
    for f in range(4):
        for d in range(depth):
            tile = field[f, d]
            j = f * depth + d
            packed = jnp.where((lane >= 4 * j) & (lane < 4 * j + 4), pltpu.roll(tile, (4 * j + 2) % width, 1), packed)
            t, p = (d // 2) * 2 + f // 2, (d % 2) * 2 + f % 2
            chosen = (sub >= 2 * p) & (sub < 2 * p + 2)
            up = pltpu.roll(tile, (2 * p) % 8, 0) if p else tile
            down = pltpu.roll(tile, (2 * p + 2) % 8, 0) if (2 * p + 2) % 8 else tile
            up_pack[t] = jnp.where(chosen, up, up_pack.get(t, 0.0))
            down_pack[t] = jnp.where(chosen, down, down_pack.get(t, 0.0))
    lane_pack[...] = packed
    for t in range(depth):
        row_pack[0, t] = up_pack[t]
        row_pack[1, t] = down_pack[t]

    def rim_copy(a, b, c):
        span = slice(depth - 2, depth) if a > 0 else slice(0, 2)
        if c != 0:
            src, dst = lane_pack, from_cols.at[(1 - a) * 3 + (1 - b), side(-c)]
        elif b == 0:
            src, dst = field.at[:, span], from_depth.at[side(-a)]
        elif a == 0:
            src, dst = row_pack.at[side(b)], from_rows.at[side(-b)]
        else:
            src, dst = row_pack.at[side(b), span], from_rows_depth.at[side(-a), side(-b)]
        return pltpu.make_async_remote_copy(
            src_ref=src,
            dst_ref=dst,
            send_sem=rim_send.at[code(a, b, c)],
            recv_sem=rim_recv.at[code(-a, -b, -c)],
            device_id=(x + b, y + c, z + a),
            device_id_type=MESH,
        )

    pl.semaphore_wait(barrier, greeted)
    for o in OFFSETS:
        pl.when(present(*o))(lambda o=o: rim_copy(*o).start())

    surf_offsets = [(b, c) for b in SIGNS for c in SIGNS if (b, c) != (0, 0)]

    def surf_present(b, c, receiving):
        yes = present(0, b, c)
        toward = -c if receiving else c
        if toward > 0:
            yes = jnp.logical_and(yes, z == 0)
        if toward < 0:
            yes = jnp.logical_and(yes, z == nz - 1)
        return yes

    def surf_copies(b, c):
        def spans(sign, size, halo, lead):
            if sign == 0:
                return slice(0, size), slice(lead, lead + size)
            if sign > 0:
                return slice(size - halo, size), slice(0, halo)
            return slice(0, halo), slice(lead + size, lead + size + halo)

        cs, cd = spans(c, cols, width, width)
        n = (b + 1) * 3 + (c + 1)
        m = (1 - b) * 3 + (1 - c)
        made = []
        for i, (src, dst, halo) in enumerate(((topo_hbm, height, STEPS), (kappa_hbm, conduct, krow))):
            rs, rd = spans(b, rows, halo, halo)
            made.append(
                pltpu.make_async_remote_copy(
                    src_ref=src.at[rs, cs],
                    dst_ref=dst.at[rd, cd],
                    send_sem=surf_send.at[i, n],
                    recv_sem=surf_recv.at[i, m],
                    device_id=(x + b, y + c, z),
                    device_id_type=MESH,
                )
            )
        return made

    def surf_start(b, c):
        for copy in surf_copies(b, c):
            copy.start()

    for o in surf_offsets:
        pl.when(surf_present(*o, False))(lambda o=o: surf_start(*o))

    for a, b, c in OFFSETS:
        pl.when(present(a, b, c))(lambda o=(-a, -b, -c): rim_copy(*o).wait_recv())
    from_low = sub < cells // 2
    from_left = (lane % 4) < 2
    for a in SIGNS:
        joined = []
        low = from_cols[(a + 1) * 3 + 1, 0]
        high = from_cols[(a + 1) * 3 + 1, 1]
        if True:
            joined.append(jnp.where(from_left, low, high))
            low = jnp.where(from_low, from_cols[(a + 1) * 3 + 2, 0], from_cols[(a + 1) * 3, 0])
            high = jnp.where(from_low, from_cols[(a + 1) * 3 + 2, 1], from_cols[(a + 1) * 3, 1])
            joined.append(jnp.where(from_left, low, high))
        for f in range(4):
            for d in range(depth) if a == 0 else (range(2) if a > 0 else range(depth - 2, depth)):
                layer = REACH + a * depth + d
                t, p = (d // 2) * 2 + f // 2, (d % 2) * 2 + f % 2
                if a == 0:
                    center, above, below = field[f, d], from_rows[0, t], from_rows[1, t]
                else:
                    center = from_depth[side(a), f, d % 2]
                    above = from_rows_depth[side(a), 0, f // 2]
                    below = from_rows_depth[side(a), 1, f // 2]
                above = pltpu.roll(above, 6 - 2 * p, 0) if p != 3 else above
                below = pltpu.roll(below, 8 - 2 * p, 0) if p else below
                j = f * depth + d
                ext[f, layer, 0:cells, 0:width] = center
                ext[f, layer, cells:, 0:width] = jnp.where(from_low, below, above)
                turn = (width - 2 - 4 * j) % width
                for r in range(2):
                    tile = pltpu.roll(joined[r], turn, 1) if turn else joined[r]
                    ext[f, layer, r * cells : (r + 1) * cells, width:] = tile

    eta = ext[3]
    gain = drag + W_ALL * eta[1:-1] + weighted(eta)
    for f in range(3):
        v = ext[f]
        out = gain * v[1:-1] - eta[1:-1] * weighted(v) - weighted(eta * v)
        image[f] = jnp.where(eta[1:-1] > 0.0, out, 0.0)
    eta1 = eta[1:-1]
    center = (slice(None), slice(0, cells), slice(0, width))
    m0 = m1 = jnp.zeros((cells, width), jnp.float32)
    for f in range(3):
        b = field[f]
        ab = image[f, 1:-1, 0:cells, 0:width]
        m0 = m0 + (b * b).sum(axis=0)
        m1 = m1 + (b * ab).sum(axis=0)
    m0, m1 = total(m0), total(m1)
    own = jnp.where(m0 > 0.0, m1 / m0, 0.0)
    sums = [jnp.zeros((cells, width), jnp.float32) for _ in range(4)]
    for f in range(3):
        v = image[f]
        b = field[f]
        ab = v[1:-1][center]
        again = (
            gain[1:-1][center] * ab
            - eta1[1:-1][center] * weighted(v)[center]
            - weighted(eta1 * v)[center]
        )
        w = ab - own * b
        aw = again - own * ab
        for i, (p, q) in enumerate(((w, b), (w, w), (w, aw), (b, aw))):
            sums[i] = sums[i] + (p * q).sum(axis=0)
    numbers = [m0, m1, own] + [total(s) for s in sums]
    spot = lax.broadcasted_iota(jnp.int32, (1, width), 1)
    line = jnp.zeros((1, width), jnp.float32)
    for i, number in enumerate(numbers):
        line = jnp.where(spot == i, number, line)
    row_out[0] = line
    first_of_plane = y * plane
    me = first_of_plane + x * nz + z
    gathered[me] = line
    top_own[0] = field[2, depth - 1]
    top_own[1] = image[2, depth, 0:cells, 0:width]
    for a, c in in_plane[1:]:
        pltpu.make_async_remote_copy(
            src_ref=row_out.at[0],
            dst_ref=gathered.at[me],
            send_sem=sum_send.at[0],
            recv_sem=sum_recv.at[0],
            device_id=(xs[a], y, zs[c]),
            device_id_type=MESH,
        ).start()

    def top_copy(k):
        return pltpu.make_async_remote_copy(
            src_ref=top_own,
            dst_ref=top_in,
            send_sem=top_send.at[k],
            recv_sem=top_recv,
            device_id=(x, y, zs[k]),
            device_id_type=MESH,
        )

    @pl.when(is_top)
    def _():
        for k in range(1, nz):
            top_copy(k).start()

    for b, c in surf_offsets:

        def arrived(b=b, c=c):
            for copy in surf_copies(-b, -c):
                copy.wait_recv()

        pl.when(surf_present(b, c, True))(arrived)
    loads[3].wait()
    start = pl.multiple_of(z * share, share)
    tall = rows + 2 * STEPS
    left_half = lax.broadcasted_iota(jnp.int32, (1, width), 1) < width // 2

    def joined_window(ref):
        wide = ref[:, pl.ds(start, share + 2 * width)].astype(jnp.float32)
        rim = jnp.where(left_half, wide[:, width + share :], wide[:, :width])
        return jnp.concatenate([wide[:, width : width + share], rim], axis=1)

    work[...] = joined_window(height)
    k = joined_window(conduct)[krow - STEPS : krow + rows + STEPS]
    span = share + width
    face_right[...] = 0.5 * (k + pltpu.roll(k, span - 1, 1))
    face_down[...] = 0.5 * (k + pltpu.roll(k, tall - 1, 0))
    row_at = x * rows - STEPS + lax.broadcasted_iota(jnp.int32, (tall, span), 0)
    lane_at = lax.broadcasted_iota(jnp.int32, (tall, span), 1)
    lane_at = jnp.where(lane_at >= span - width // 2, lane_at - span, lane_at)
    col_at = y * cols + z * share + lane_at
    inside[...] = jnp.where(
        (row_at >= 0) & (row_at < rows * nx) & (col_at >= 0) & (col_at < cols * ny), time_step, 0.0
    )

    def diffuse(_, carry):
        h = work[...]
        s = pltpu.roll(h, span - 1, 1) - h
        along = face_right[...] * s * lax.rsqrt(1.0 + s * s)
        s = pltpu.roll(h, tall - 1, 0) - h
        across = face_down[...] * s * lax.rsqrt(1.0 + s * s)
        change = along - pltpu.roll(along, 1, 1) + across - pltpu.roll(across, 1, 0)
        work[...] = h + inside[...] * change
        return carry

    lax.fori_loop(0, EARLY, diffuse, 0)

    most = gathered.at[pl.ds(0, plane - 1)]
    pltpu.make_async_copy(most, most, sum_recv.at[0]).wait()
    whole_plane = gathered.at[pl.ds(first_of_plane, plane)]
    for k in range(1, ny):
        pltpu.make_async_remote_copy(
            src_ref=whole_plane,
            dst_ref=whole_plane,
            send_sem=sum_send.at[1],
            recv_sem=sum_recv.at[1],
            device_id=(x, ys[k], z),
            device_id_type=MESH,
        ).start()

    lax.fori_loop(EARLY, STEPS, diffuse, 0)

    @pl.when(jnp.logical_not(is_top))
    def _():
        top_copy(1).wait_recv()
        top_own[...] = top_in[...]

    cell_at = lax.broadcasted_iota(jnp.int32, (width, share), 0) * ratio_c
    col = z * share + lax.broadcasted_iota(jnp.int32, (width, share), 1)
    pick = jnp.where((col >= cell_at) & (col < cell_at + ratio_c), 1.0, 0.0)
    spread = picked(top_own[...].reshape(2 * cells, width), pick.astype(jnp.bfloat16))

    for o in OFFSETS:
        pl.when(present(*o))(lambda o=o: rim_copy(*o).wait_send())
    for b, c in surf_offsets:

        def sent(b=b, c=c):
            for copy in surf_copies(b, c):
                copy.wait_send()

        pl.when(surf_present(b, c, False))(sent)

    @pl.when(is_top)
    def _():
        for k in range(1, nz):
            top_copy(k).wait_send()

    rest = gathered.at[pl.ds(0, plane * (ny - 1))]
    pltpu.make_async_copy(most, most, sum_send.at[0]).wait()
    pltpu.make_async_copy(rest, rest, sum_send.at[1]).wait()
    pltpu.make_async_copy(rest, rest, sum_recv.at[1]).wait()

    table = gathered[...].reshape(count, width)
    m0, m1, own, e, ww, waw, baw = [table[:, i : i + 1] for i in range(7)]
    rr = m0.sum(axis=0, keepdims=True)
    bab = m1.sum(axis=0, keepdims=True)
    mean = bab / rr
    off = own - mean
    s2 = (ww + off * (2.0 * e + off * m0)).sum(axis=0, keepdims=True)
    q = (waw + off * (ww + own * e + baw + off * m1)).sum(axis=0, keepdims=True)
    alpha0 = rr / bab
    beta = s2 / (mean * bab)
    alpha1 = s2 / (q - s2 * s2 / bab)
    on_b = alpha0 + alpha1 * (1.0 + beta)
    on_ab = -alpha1 * alpha0
    for f in range(3):
        velocity_ref[f] = on_b * field[f] + on_ab * image[f, 1:-1, 0:cells, 0:width]
    rise = (STEPS * time_step) * (on_b * spread[:cells] + on_ab * spread[cells:])
    rise = jnp.broadcast_to(rise[:, None, :], (cells, ratio_r, share)).reshape(rows, share)
    surface_ref[...] = work[STEPS : STEPS + rows, 0:share] + rise


def local(sizes, body_force, viscosity, topography, kappa):
    depth, cells, width = viscosity.shape
    rows, cols = topography.shape
    nx, ny, nz = sizes
    count = nx * ny * nz
    share = cols // nz
    f32 = jnp.float32
    dma = pltpu.SemaphoreType.DMA
    return pl.pallas_call(
        functools.partial(kernel, sizes),
        out_shape=(
            jax.ShapeDtypeStruct(body_force.shape, f32),
            jax.ShapeDtypeStruct((rows, share), f32),
        ),
        in_specs=[pl.BlockSpec(memory_space=pltpu.HBM)] * 4,
        out_specs=[pl.BlockSpec(memory_space=pltpu.VMEM)] * 2,
        scratch_shapes=[
            pltpu.VMEM((4, depth, cells, width), f32),
            pltpu.VMEM((cells, width), f32),
            pltpu.VMEM((2, depth, cells, width), f32),
            pltpu.VMEM((2, 4, REACH, cells, width), f32),
            pltpu.VMEM((2, depth, cells, width), f32),
            pltpu.VMEM((2, 2, 2, cells, width), f32),
            pltpu.VMEM((9, 2, cells, width), f32),
            pltpu.VMEM((4, depth + 2 * REACH, 2 * cells, 2 * width), f32),
            pltpu.VMEM((3, depth + 2 * REACH - 2, 2 * cells, 2 * width), f32),
            pltpu.VMEM((rows + 2 * STEPS, cols + 2 * width), f32),
            pltpu.VMEM((rows + 32, cols + 2 * width), kappa.dtype),
            pltpu.VMEM((rows + 2 * STEPS, share + width), f32),
            pltpu.VMEM((rows + 2 * STEPS, share + width), f32),
            pltpu.VMEM((rows + 2 * STEPS, share + width), f32),
            pltpu.VMEM((rows + 2 * STEPS, share + width), f32),
            pltpu.VMEM((1, 1, width), f32),
            pltpu.VMEM((count, 1, width), f32),
            pltpu.VMEM((2, cells, width), f32),
            pltpu.VMEM((2, cells, width), f32),
            dma((4,)),
            dma((27,)),
            dma((27,)),
            dma((2, 9)),
            dma((2, 9)),
            dma((2,)),
            dma((2,)),
            dma((nz,)),
            dma,
        ],
        compiler_params=pltpu.CompilerParams(
            collective_id=0, has_side_effects=True, vmem_limit_bytes=32 * 1024 * 1024
        ),
    )(*[pltpu.with_memory_space_constraint(one, pltpu.HBM) for one in (body_force, viscosity, topography, kappa)])


def solution(mesh):
    sizes = tuple(mesh.shape[axis] for axis in ("gx", "gy", "gz"))
    in_specs = (P(None, "gz", "gx", "gy"), P("gz", "gx", "gy"), P("gx", "gy"), P("gx", "gy"))
    out_specs = (P(None, "gz", "gx", "gy"), P("gx", ("gy", "gz")))
    return jax.shard_map(
        functools.partial(local, sizes), mesh=mesh, in_specs=in_specs, out_specs=out_specs, check_vma=False
    )
```

```python
import functools

import jax
import jax.numpy as jnp
from jax import lax
from jax.experimental import pallas as pl
from jax.experimental.pallas import tpu as pltpu
from jax.sharding import PartitionSpec as P

STEPS = 8
REACH = 2

drag = 1.0
time_step = 1.0
load_gain = 4.0

W_FACE = 0.5
W_EDGE = 0.25
W_CORNER = 0.5 / 3.0
W_ALL = 6 * W_FACE + 12 * W_EDGE + 8 * W_CORNER

MESH = pl.DeviceIdType.MESH
SIGNS = (-1, 0, 1)
OFFSETS = sorted(
    [(a, b, c) for a in SIGNS for b in SIGNS for c in SIGNS if (a, b, c) != (0, 0, 0)],
    key=lambda o: (abs(o[0]) + abs(o[1]) + abs(o[2]), abs(o[2])),
)


def side(sign):
    return 0 if sign < 0 else 1


def code(a, b, c):
    return (a + 1) * 9 + (b + 1) * 3 + (c + 1)


def weighted(u):
    rows, lanes = u.shape[1:]
    beside = pltpu.roll(u, 1, 2) + pltpu.roll(u, lanes - 1, 2)
    near = W_FACE * u + W_EDGE * beside
    far = W_EDGE * u + W_CORNER * beside
    level = W_FACE * beside[1:-1] + (near[:-2] + near[2:])
    next_row = near[1:-1] + (far[:-2] + far[2:])
    return level + (pltpu.roll(next_row, 1, 1) + pltpu.roll(next_row, rows - 1, 1))


def picked(x, choice):
    parts = []
    for _ in range(3):
        part = x.astype(jnp.bfloat16)
        parts.append(part.astype(jnp.float32))
        x = x - parts[-1]
    rows = x.shape[0]
    stacked = jnp.concatenate(parts, axis=0).astype(jnp.bfloat16)
    out = jnp.dot(stacked, choice, preferred_element_type=jnp.float32)
    return out[:rows] + (out[rows : 2 * rows] + out[2 * rows :])


def total(x):
    x = x.reshape((-1,) + x.shape[-2:]).sum(axis=0)
    return x.sum(axis=(0, 1), keepdims=True)


def kernel(
    sizes,
    force_hbm,
    visc_hbm,
    topo_hbm,
    kappa_hbm,
    velocity_ref,
    surface_ref,
    field,
    lane_pack,
    row_pack,
    from_depth,
    from_rows,
    from_rows_depth,
    from_cols,
    ext,
    image,
    spreader,
    height,
    conduct,
    work,
    face_right,
    face_down,
    inside,
    row_out,
    gathered,
    top_own,
    top_in,
    load_sem,
    rim_send,
    rim_recv,
    surf_send,
    surf_recv,
    sum_send,
    sum_recv,
    top_send,
    top_recv,
):
    nx, ny, nz = sizes
    count = nx * ny * nz
    x, y, z = lax.axis_index("gx"), lax.axis_index("gy"), lax.axis_index("gz")
    depth, cells, width = field.shape[1:]
    rows, cols = topo_hbm.shape
    share = cols // nz
    krow = 16

    xs = [lax.rem(x + k, nx) for k in range(nx)]
    ys = [lax.rem(y + k, ny) for k in range(ny)]
    zs = [lax.rem(z + k, nz) for k in range(nz)]
    others = [(a, b, c) for a in range(nx) for b in range(ny) for c in range(nz)][1:]
    others.sort(key=lambda o: -(min(o[0], nx - o[0]) + min(o[1], ny - o[1]) + min(o[2], nz - o[2])))
    is_top = z == nz - 1

    loads = [
        pltpu.make_async_copy(topo_hbm, height.at[STEPS : STEPS + rows, width : width + cols], load_sem.at[0]),
        pltpu.make_async_copy(force_hbm, field.at[0:3], load_sem.at[1]),
        pltpu.make_async_copy(visc_hbm, field.at[3], load_sem.at[2]),
        pltpu.make_async_copy(kappa_hbm, conduct.at[krow : krow + rows, width : width + cols], load_sem.at[3]),
    ]
    for copy in loads:
        copy.start()

    for ref in (from_depth, from_rows, from_rows_depth, from_cols):
        ref[...] = jnp.zeros_like(ref)
    height[0:STEPS, :] = jnp.zeros((STEPS, height.shape[1]), height.dtype)
    height[STEPS + rows :, :] = jnp.zeros((STEPS, height.shape[1]), height.dtype)
    height[STEPS : STEPS + rows, 0:width] = jnp.zeros((rows, width), height.dtype)
    height[STEPS : STEPS + rows, width + cols :] = jnp.zeros((rows, width), height.dtype)
    conduct[0:krow, :] = jnp.zeros((krow, conduct.shape[1]), conduct.dtype)
    conduct[krow + rows :, :] = jnp.zeros((krow, conduct.shape[1]), conduct.dtype)
    conduct[krow : krow + rows, 0:width] = jnp.zeros((rows, width), conduct.dtype)
    conduct[krow : krow + rows, width + cols :] = jnp.zeros((rows, width), conduct.dtype)

    barrier = pltpu.get_barrier_semaphore()
    for a, b, c in others:
        pl.semaphore_signal(barrier, inc=1, device_id=(xs[a], ys[b], zs[c]), device_id_type=MESH)

    ratio_r, ratio_c = rows // cells, cols // width
    at = lax.broadcasted_iota(jnp.int32, (cols, width), 0)
    first = lax.broadcasted_iota(jnp.int32, (cols, width), 1) * ratio_c
    pick = jnp.where((at >= first) & (at < first + ratio_c), 1.0, 0.0).astype(jnp.bfloat16)

    def present(a, b, c):
        yes = None
        for sign, at_, size in ((a, z, nz), (b, x, nx), (c, y, ny)):
            if sign:
                one = at_ > 0 if sign < 0 else at_ < size - 1
                yes = one if yes is None else jnp.logical_and(yes, one)
        return yes

    loads[0].wait()
    by_rows = height[STEPS : STEPS + rows, width : width + cols].reshape(cells, ratio_r, cols).sum(axis=1)
    load = picked(by_rows, pick) * (1.0 / (ratio_r * ratio_c))
    loads[1].wait()
    loads[2].wait()
    field[2, depth - 1] = field[2, depth - 1] + jnp.where(is_top, -load_gain * load, 0.0)

    lane = lax.broadcasted_iota(jnp.int32, (cells, width), 1)
    sub = lax.broadcasted_iota(jnp.int32, (cells, width), 0)
    packed = jnp.zeros((cells, width), jnp.float32)
    up_pack, down_pack = {}, {}
    for f in range(4):
        for d in range(depth):
            tile = field[f, d]
            j = f * depth + d
            packed = jnp.where((lane >= 4 * j) & (lane < 4 * j + 4), pltpu.roll(tile, (4 * j + 2) % width, 1), packed)
            t, p = (d // 2) * 2 + f // 2, (d % 2) * 2 + f % 2
            chosen = (sub >= 2 * p) & (sub < 2 * p + 2)
            up = pltpu.roll(tile, (2 * p) % 8, 0) if p else tile
            down = pltpu.roll(tile, (2 * p + 2) % 8, 0) if (2 * p + 2) % 8 else tile
            up_pack[t] = jnp.where(chosen, up, up_pack.get(t, 0.0))
            down_pack[t] = jnp.where(chosen, down, down_pack.get(t, 0.0))
    lane_pack[...] = packed
    for t in range(depth):
        row_pack[0, t] = up_pack[t]
        row_pack[1, t] = down_pack[t]

    def rim_copy(a, b, c):
        span = slice(depth - 2, depth) if a > 0 else slice(0, 2)
        if c != 0:
            src, dst = lane_pack, from_cols.at[(1 - a) * 3 + (1 - b), side(-c)]
        elif b == 0:
            src, dst = field.at[:, span], from_depth.at[side(-a)]
        elif a == 0:
            src, dst = row_pack.at[side(b)], from_rows.at[side(-b)]
        else:
            src, dst = row_pack.at[side(b), span], from_rows_depth.at[side(-a), side(-b)]
        return pltpu.make_async_remote_copy(
            src_ref=src,
            dst_ref=dst,
            send_sem=rim_send.at[code(a, b, c)],
            recv_sem=rim_recv.at[code(-a, -b, -c)],
            device_id=(x + b, y + c, z + a),
            device_id_type=MESH,
        )

    pl.semaphore_wait(barrier, count - 1)
    for o in OFFSETS:
        pl.when(present(*o))(lambda o=o: rim_copy(*o).start())

    surf_offsets = [(b, c) for b in SIGNS for c in SIGNS if (b, c) != (0, 0)]

    def surf_present(b, c, receiving):
        yes = present(0, b, c)
        toward = -c if receiving else c
        if toward > 0:
            yes = jnp.logical_and(yes, z == 0)
        if toward < 0:
            yes = jnp.logical_and(yes, z == nz - 1)
        return yes

    def surf_copies(b, c):
        def spans(sign, size, halo, lead):
            if sign == 0:
                return slice(0, size), slice(lead, lead + size)
            if sign > 0:
                return slice(size - halo, size), slice(0, halo)
            return slice(0, halo), slice(lead + size, lead + size + halo)

        cs, cd = spans(c, cols, width, width)
        n = (b + 1) * 3 + (c + 1)
        m = (1 - b) * 3 + (1 - c)
        made = []
        for i, (src, dst, halo) in enumerate(((topo_hbm, height, STEPS), (kappa_hbm, conduct, krow))):
            rs, rd = spans(b, rows, halo, halo)
            made.append(
                pltpu.make_async_remote_copy(
                    src_ref=src.at[rs, cs],
                    dst_ref=dst.at[rd, cd],
                    send_sem=surf_send.at[i, n],
                    recv_sem=surf_recv.at[i, m],
                    device_id=(x + b, y + c, z),
                    device_id_type=MESH,
                )
            )
        return made

    def surf_start(b, c):
        for copy in surf_copies(b, c):
            copy.start()

    for o in surf_offsets:
        pl.when(surf_present(*o, False))(lambda o=o: surf_start(*o))

    tall, span = rows + 2 * STEPS, share + width
    row_at = x * rows - STEPS + lax.broadcasted_iota(jnp.int32, (tall, span), 0)
    lane_at = lax.broadcasted_iota(jnp.int32, (tall, span), 1)
    lane_at = jnp.where(lane_at >= span - width // 2, lane_at - span, lane_at)
    col_at = y * cols + z * share + lane_at
    inside[...] = jnp.where(
        (row_at >= 0) & (row_at < rows * nx) & (col_at >= 0) & (col_at < cols * ny), time_step, 0.0
    )

    cell_at = lax.broadcasted_iota(jnp.int32, (width, share), 0) * ratio_c
    col = z * share + lax.broadcasted_iota(jnp.int32, (width, share), 1)
    spreader[...] = jnp.where((col >= cell_at) & (col < cell_at + ratio_c), 1.0, 0.0).astype(jnp.bfloat16)
    for o in OFFSETS:
        pl.when(present(*o))(lambda o=o: rim_copy(*o).wait_send())
    for b, c in surf_offsets:

        def sent(b=b, c=c):
            for copy in surf_copies(b, c):
                copy.wait_send()

        pl.when(surf_present(b, c, False))(sent)

    for a, b, c in OFFSETS:
        pl.when(present(a, b, c))(lambda o=(-a, -b, -c): rim_copy(*o).wait_recv())
    from_low = sub < cells // 2
    from_left = (lane % 4) < 2
    for a in SIGNS:
        joined = []
        low = from_cols[(a + 1) * 3 + 1, 0]
        high = from_cols[(a + 1) * 3 + 1, 1]
        if True:
            joined.append(jnp.where(from_left, low, high))
            low = jnp.where(from_low, from_cols[(a + 1) * 3 + 2, 0], from_cols[(a + 1) * 3, 0])
            high = jnp.where(from_low, from_cols[(a + 1) * 3 + 2, 1], from_cols[(a + 1) * 3, 1])
            joined.append(jnp.where(from_left, low, high))
        for f in range(4):
            for d in range(depth) if a == 0 else (range(2) if a > 0 else range(depth - 2, depth)):
                layer = REACH + a * depth + d
                t, p = (d // 2) * 2 + f // 2, (d % 2) * 2 + f % 2
                if a == 0:
                    center, above, below = field[f, d], from_rows[0, t], from_rows[1, t]
                else:
                    center = from_depth[side(a), f, d % 2]
                    above = from_rows_depth[side(a), 0, f // 2]
                    below = from_rows_depth[side(a), 1, f // 2]
                above = pltpu.roll(above, 6 - 2 * p, 0) if p != 3 else above
                below = pltpu.roll(below, 8 - 2 * p, 0) if p else below
                j = f * depth + d
                ext[f, layer, 0:cells, 0:width] = center
                ext[f, layer, cells:, 0:width] = jnp.where(from_low, below, above)
                turn = (width - 2 - 4 * j) % width
                for r in range(2):
                    tile = pltpu.roll(joined[r], turn, 1) if turn else joined[r]
                    ext[f, layer, r * cells : (r + 1) * cells, width:] = tile

    eta = ext[3]
    gain = drag + W_ALL * eta[1:-1] + weighted(eta)
    for f in range(3):
        v = ext[f]
        out = gain * v[1:-1] - eta[1:-1] * weighted(v) - weighted(eta * v)
        image[f] = jnp.where(eta[1:-1] > 0.0, out, 0.0)
    eta1 = eta[1:-1]
    center = (slice(None), slice(0, cells), slice(0, width))
    m0 = m1 = jnp.zeros((cells, width), jnp.float32)
    for f in range(3):
        b = field[f]
        ab = image[f, 1:-1, 0:cells, 0:width]
        m0 = m0 + (b * b).sum(axis=0)
        m1 = m1 + (b * ab).sum(axis=0)
    m0, m1 = total(m0), total(m1)
    own = jnp.where(m0 > 0.0, m1 / m0, 0.0)
    sums = [jnp.zeros((cells, width), jnp.float32) for _ in range(4)]
    for f in range(3):
        v = image[f]
        b = field[f]
        ab = v[1:-1][center]
        again = (
            gain[1:-1][center] * ab
            - eta1[1:-1][center] * weighted(v)[center]
            - weighted(eta1 * v)[center]
        )
        w = ab - own * b
        aw = again - own * ab
        for i, (p, q) in enumerate(((w, b), (w, w), (w, aw), (b, aw))):
            sums[i] = sums[i] + (p * q).sum(axis=0)
    numbers = [m0, m1, own] + [total(s) for s in sums]
    spot = lax.broadcasted_iota(jnp.int32, (1, width), 1)
    line = jnp.zeros((1, width), jnp.float32)
    for i, number in enumerate(numbers):
        line = jnp.where(spot == i, number, line)
    row_out[0] = line
    me = (x * ny + y) * nz + z
    gathered[me] = line
    top_own[0] = field[2, depth - 1]
    top_own[1] = image[2, depth, 0:cells, 0:width]
    for a, b, c in others:
        pltpu.make_async_remote_copy(
            src_ref=row_out.at[0],
            dst_ref=gathered.at[me],
            send_sem=sum_send,
            recv_sem=sum_recv,
            device_id=(xs[a], ys[b], zs[c]),
            device_id_type=MESH,
        ).start()

    def top_copy(k):
        return pltpu.make_async_remote_copy(
            src_ref=top_own,
            dst_ref=top_in,
            send_sem=top_send.at[k],
            recv_sem=top_recv,
            device_id=(x, y, zs[k]),
            device_id_type=MESH,
        )

    @pl.when(is_top)
    def _():
        for k in range(1, nz):
            top_copy(k).start()

    for b, c in surf_offsets:

        def arrived(b=b, c=c):
            for copy in surf_copies(-b, -c):
                copy.wait_recv()

        pl.when(surf_present(b, c, True))(arrived)
    loads[3].wait()
    start = pl.multiple_of(z * share, share)
    left_half = lax.broadcasted_iota(jnp.int32, (1, width), 1) < width // 2

    def joined_window(ref):
        wide = ref[:, pl.ds(start, share + 2 * width)].astype(jnp.float32)
        rim = jnp.where(left_half, wide[:, width + share :], wide[:, :width])
        return jnp.concatenate([wide[:, width : width + share], rim], axis=1)

    work[...] = joined_window(height)
    k = joined_window(conduct)[krow - STEPS : krow + rows + STEPS]
    face_right[...] = 0.5 * (k + pltpu.roll(k, span - 1, 1))
    face_down[...] = 0.5 * (k + pltpu.roll(k, tall - 1, 0))
    def stepped():
        h = work[...]
        s = pltpu.roll(h, span - 1, 1) - h
        along = face_right[...] * s * lax.rsqrt(1.0 + s * s)
        s = pltpu.roll(h, tall - 1, 0) - h
        across = face_down[...] * s * lax.rsqrt(1.0 + s * s)
        change = along - pltpu.roll(along, 1, 1) + across - pltpu.roll(across, 1, 0)
        return h + inside[...] * change

    def diffuse(_, carry):
        for _ in range(2):
            work[...] = stepped()
        return carry

    lax.fori_loop(0, (STEPS - 1) // 2, diffuse, 0)
    for _ in range((STEPS - 1) % 2):
        work[...] = stepped()
    surface_ref[...] = stepped()[STEPS : STEPS + rows, 0:share]

    @pl.when(jnp.logical_not(is_top))
    def _():
        top_copy(1).wait_recv()
        top_own[...] = top_in[...]

    spread = picked(top_own[...].reshape(2 * cells, width), spreader[...])

    @pl.when(is_top)
    def _():
        for k in range(1, nz):
            top_copy(k).wait_send()

    most = gathered.at[pl.ds(0, count - 1)]
    pltpu.make_async_copy(most, most, sum_send).wait()
    pltpu.make_async_copy(most, most, sum_recv).wait()

    table = gathered[...].reshape(count, width)
    m0, m1, own, e, ww, waw, baw = [table[:, i : i + 1] for i in range(7)]
    rr = m0.sum(axis=0, keepdims=True)
    bab = m1.sum(axis=0, keepdims=True)
    mean = bab / rr
    off = own - mean
    s2 = (ww + off * (2.0 * e + off * m0)).sum(axis=0, keepdims=True)
    q = (waw + off * (ww + own * e + baw + off * m1)).sum(axis=0, keepdims=True)
    alpha0 = rr / bab
    beta = s2 / (mean * bab)
    alpha1 = s2 / (q - s2 * s2 / bab)
    on_b = alpha0 + alpha1 * (1.0 + beta)
    on_ab = -alpha1 * alpha0
    for f in range(3):
        velocity_ref[f] = on_b * field[f] + on_ab * image[f, 1:-1, 0:cells, 0:width]
    rise = (STEPS * time_step) * (on_b * spread[:cells] + on_ab * spread[cells:])
    rise = jnp.broadcast_to(rise[:, None, :], (cells, ratio_r, share)).reshape(rows, share)
    surface_ref[...] = surface_ref[...] + rise


def local(sizes, body_force, viscosity, topography, kappa):
    depth, cells, width = viscosity.shape
    rows, cols = topography.shape
    nx, ny, nz = sizes
    count = nx * ny * nz
    share = cols // nz
    f32 = jnp.float32
    dma = pltpu.SemaphoreType.DMA
    return pl.pallas_call(
        functools.partial(kernel, sizes),
        out_shape=(
            jax.ShapeDtypeStruct(body_force.shape, f32),
            jax.ShapeDtypeStruct((rows, share), f32),
        ),
        in_specs=[pl.BlockSpec(memory_space=pltpu.HBM)] * 4,
        out_specs=[pl.BlockSpec(memory_space=pltpu.VMEM)] * 2,
        scratch_shapes=[
            pltpu.VMEM((4, depth, cells, width), f32),
            pltpu.VMEM((cells, width), f32),
            pltpu.VMEM((2, depth, cells, width), f32),
            pltpu.VMEM((2, 4, REACH, cells, width), f32),
            pltpu.VMEM((2, depth, cells, width), f32),
            pltpu.VMEM((2, 2, 2, cells, width), f32),
            pltpu.VMEM((9, 2, cells, width), f32),
            pltpu.VMEM((4, depth + 2 * REACH, 2 * cells, 2 * width), f32),
            pltpu.VMEM((3, depth + 2 * REACH - 2, 2 * cells, 2 * width), f32),
            pltpu.VMEM((width, share), jnp.bfloat16),
            pltpu.VMEM((rows + 2 * STEPS, cols + 2 * width), f32),
            pltpu.VMEM((rows + 32, cols + 2 * width), kappa.dtype),
            pltpu.VMEM((rows + 2 * STEPS, share + width), f32),
            pltpu.VMEM((rows + 2 * STEPS, share + width), f32),
            pltpu.VMEM((rows + 2 * STEPS, share + width), f32),
            pltpu.VMEM((rows + 2 * STEPS, share + width), f32),
            pltpu.VMEM((1, 1, width), f32),
            pltpu.VMEM((count, 1, width), f32),
            pltpu.VMEM((2, cells, width), f32),
            pltpu.VMEM((2, cells, width), f32),
            dma((4,)),
            dma((27,)),
            dma((27,)),
            dma((2, 9)),
            dma((2, 9)),
            dma,
            dma,
            dma((nz,)),
            dma,
        ],
        compiler_params=pltpu.CompilerParams(
            collective_id=0, has_side_effects=True, vmem_limit_bytes=32 * 1024 * 1024
        ),
    )(*[pltpu.with_memory_space_constraint(one, pltpu.HBM) for one in (body_force, viscosity, topography, kappa)])


def solution(mesh):
    sizes = tuple(mesh.shape[axis] for axis in ("gx", "gy", "gz"))
    in_specs = (P(None, "gz", "gx", "gy"), P("gz", "gx", "gy"), P("gx", "gy"), P("gx", "gy"))
    out_specs = (P(None, "gz", "gx", "gy"), P("gx", ("gy", "gz")))
    return jax.shard_map(
        functools.partial(local, sizes), mesh=mesh, in_specs=in_specs, out_specs=out_specs, check_vma=False
    )
```

```python
import functools

import jax
import jax.numpy as jnp
from jax import lax
from jax.experimental import pallas as pl
from jax.experimental.pallas import tpu as pltpu
from jax.sharding import PartitionSpec as P

STEPS = 8
REACH = 2

drag = 1.0
time_step = 1.0
load_gain = 4.0

W_FACE = 0.5
W_EDGE = 0.25
W_CORNER = 0.5 / 3.0
W_ALL = 6 * W_FACE + 12 * W_EDGE + 8 * W_CORNER

MESH = pl.DeviceIdType.MESH
SIGNS = (-1, 0, 1)
OFFSETS = sorted(
    [(a, b, c) for a in SIGNS for b in SIGNS for c in SIGNS if (a, b, c) != (0, 0, 0)],
    key=lambda o: (abs(o[0]) + abs(o[1]) + abs(o[2]), abs(o[2])),
)


def side(sign):
    return 0 if sign < 0 else 1


def code(a, b, c):
    return (a + 1) * 9 + (b + 1) * 3 + (c + 1)


def weighted(layers):
    held = []
    for u in layers:
        rows, lanes = u.shape
        beside = pltpu.roll(u, 1, 1) + pltpu.roll(u, lanes - 1, 1)
        held.append((W_FACE * beside, W_FACE * u + W_EDGE * beside, W_EDGE * u + W_CORNER * beside))
        if len(held) == 3:
            (_, near0, far0), (level, near1, _), (_, near2, far2) = held
            level = level + (near0 + near2)
            next_row = near1 + (far0 + far2)
            yield level + (pltpu.roll(next_row, 1, 0) + pltpu.roll(next_row, rows - 1, 0))
            held.pop(0)


def picked(x, choice):
    parts = []
    for _ in range(3):
        part = x.astype(jnp.bfloat16)
        parts.append(part.astype(jnp.float32))
        x = x - parts[-1]
    rows = x.shape[0]
    stacked = jnp.concatenate(parts, axis=0).astype(jnp.bfloat16)
    out = jnp.dot(stacked, choice, preferred_element_type=jnp.float32)
    return out[:rows] + (out[rows : 2 * rows] + out[2 * rows :])


def total(x):
    return x.sum(axis=(0, 1), keepdims=True)


def kernel(
    sizes,
    force_hbm,
    visc_hbm,
    topo_hbm,
    kappa_hbm,
    velocity_ref,
    surface_ref,
    field,
    lane_pack,
    row_pack,
    from_depth,
    from_rows,
    from_rows_depth,
    from_cols,
    ext,
    image,
    gain,
    again,
    spreader,
    height,
    conduct,
    work,
    face_right,
    face_down,
    inside,
    row_out,
    gathered,
    top_own,
    top_in,
    load_sem,
    rim_send,
    rim_recv,
    surf_send,
    surf_recv,
    sum_send,
    sum_recv,
    top_send,
    top_recv,
):
    nx, ny, nz = sizes
    count = nx * ny * nz
    x, y, z = lax.axis_index("gx"), lax.axis_index("gy"), lax.axis_index("gz")
    depth, cells, width = field.shape[1:]
    rows, cols = topo_hbm.shape
    share = cols // nz
    krow = 16

    xs = [lax.rem(x + k, nx) for k in range(nx)]
    ys = [lax.rem(y + k, ny) for k in range(ny)]
    zs = [lax.rem(z + k, nz) for k in range(nz)]
    others = [(a, b, c) for a in range(nx) for b in range(ny) for c in range(nz)][1:]
    others.sort(key=lambda o: -(min(o[0], nx - o[0]) + min(o[1], ny - o[1]) + min(o[2], nz - o[2])))
    is_top = z == nz - 1

    loads = [
        pltpu.make_async_copy(topo_hbm, height.at[STEPS : STEPS + rows, width : width + cols], load_sem.at[0]),
        pltpu.make_async_copy(force_hbm, field.at[0:3], load_sem.at[1]),
        pltpu.make_async_copy(visc_hbm, field.at[3], load_sem.at[2]),
        pltpu.make_async_copy(kappa_hbm, conduct.at[krow : krow + rows, width : width + cols], load_sem.at[3]),
    ]
    for copy in loads:
        copy.start()

    for ref in (from_depth, from_rows, from_rows_depth, from_cols):
        ref[...] = jnp.zeros_like(ref)
    height[0:STEPS, :] = jnp.zeros((STEPS, height.shape[1]), height.dtype)
    height[STEPS + rows :, :] = jnp.zeros((STEPS, height.shape[1]), height.dtype)
    height[STEPS : STEPS + rows, 0:width] = jnp.zeros((rows, width), height.dtype)
    height[STEPS : STEPS + rows, width + cols :] = jnp.zeros((rows, width), height.dtype)
    conduct[0:krow, :] = jnp.zeros((krow, conduct.shape[1]), conduct.dtype)
    conduct[krow + rows :, :] = jnp.zeros((krow, conduct.shape[1]), conduct.dtype)
    conduct[krow : krow + rows, 0:width] = jnp.zeros((rows, width), conduct.dtype)
    conduct[krow : krow + rows, width + cols :] = jnp.zeros((rows, width), conduct.dtype)

    barrier = pltpu.get_barrier_semaphore()
    for a, b, c in others:
        pl.semaphore_signal(barrier, inc=1, device_id=(xs[a], ys[b], zs[c]), device_id_type=MESH)

    ratio_r, ratio_c = rows // cells, cols // width
    at = lax.broadcasted_iota(jnp.int32, (cols, width), 0)
    first = lax.broadcasted_iota(jnp.int32, (cols, width), 1) * ratio_c
    pick = jnp.where((at >= first) & (at < first + ratio_c), 1.0, 0.0).astype(jnp.bfloat16)

    def present(a, b, c):
        yes = None
        for sign, at_, size in ((a, z, nz), (b, x, nx), (c, y, ny)):
            if sign:
                one = at_ > 0 if sign < 0 else at_ < size - 1
                yes = one if yes is None else jnp.logical_and(yes, one)
        return yes

    loads[1].wait()
    loads[2].wait()
    lane = lax.broadcasted_iota(jnp.int32, (cells, width), 1)
    sub = lax.broadcasted_iota(jnp.int32, (cells, width), 0)

    def in_lane_pack(f, d, tile, packed):
        j = f * depth + d
        return jnp.where((lane >= 4 * j) & (lane < 4 * j + 4), pltpu.roll(tile, (4 * j + 2) % width, 1), packed)

    def in_row_pack(f, d, tile, packed, first_row):
        p = (d % 2) * 2 + f % 2
        turn = (2 * p - first_row) % cells
        return jnp.where((sub >= 2 * p) & (sub < 2 * p + 2), pltpu.roll(tile, turn, 0) if turn else tile, packed)

    packed = jnp.zeros((cells, width), jnp.float32)
    for f in range(4):
        for d in range(depth):
            packed = in_lane_pack(f, d, field[f, d], packed)
    for t in range(depth):
        for i, first_row in enumerate((0, cells - 2)):
            rim = jnp.zeros((cells, width), jnp.float32)
            for d in (t // 2 * 2, t // 2 * 2 + 1):
                for f in (t % 2 * 2, t % 2 * 2 + 1):
                    rim = in_row_pack(f, d, field[f, d], rim, first_row)
            row_pack[i, t] = rim

    loads[0].wait()
    by_rows = height[STEPS : STEPS + rows, width : width + cols].reshape(cells, ratio_r, cols).sum(axis=1)
    load = picked(by_rows, pick) * (1.0 / (ratio_r * ratio_c))
    loaded = field[2, depth - 1] + jnp.where(is_top, -load_gain * load, 0.0)
    field[2, depth - 1] = loaded
    lane_pack[...] = in_lane_pack(2, depth - 1, loaded, packed)
    for i, first_row in enumerate((0, cells - 2)):
        row_pack[i, depth - 1] = in_row_pack(2, depth - 1, loaded, row_pack[i, depth - 1], first_row)

    def rim_copy(a, b, c):
        span = slice(depth - 2, depth) if a > 0 else slice(0, 2)
        if c != 0:
            src, dst = lane_pack, from_cols.at[(1 - a) * 3 + (1 - b), side(-c)]
        elif b == 0:
            src, dst = field.at[:, span], from_depth.at[side(-a)]
        elif a == 0:
            src, dst = row_pack.at[side(b)], from_rows.at[side(-b)]
        else:
            src, dst = row_pack.at[side(b), span], from_rows_depth.at[side(-a), side(-b)]
        return pltpu.make_async_remote_copy(
            src_ref=src,
            dst_ref=dst,
            send_sem=rim_send.at[code(a, b, c)],
            recv_sem=rim_recv.at[code(-a, -b, -c)],
            device_id=(x + b, y + c, z + a),
            device_id_type=MESH,
        )

    pl.semaphore_wait(barrier, count - 1)
    for o in OFFSETS:
        pl.when(present(*o))(lambda o=o: rim_copy(*o).start())

    surf_offsets = [(b, c) for b in SIGNS for c in SIGNS if (b, c) != (0, 0)]

    def surf_present(b, c, receiving):
        yes = present(0, b, c)
        toward = -c if receiving else c
        if toward > 0:
            yes = jnp.logical_and(yes, z == 0)
        if toward < 0:
            yes = jnp.logical_and(yes, z == nz - 1)
        return yes

    def surf_copies(b, c):
        def spans(sign, size, halo, lead):
            if sign == 0:
                return slice(0, size), slice(lead, lead + size)
            if sign > 0:
                return slice(size - halo, size), slice(0, halo)
            return slice(0, halo), slice(lead + size, lead + size + halo)

        cs, cd = spans(c, cols, width, width)
        n = (b + 1) * 3 + (c + 1)
        m = (1 - b) * 3 + (1 - c)
        made = []
        for i, (src, dst, halo) in enumerate(((topo_hbm, height, STEPS), (kappa_hbm, conduct, krow))):
            rs, rd = spans(b, rows, halo, halo)
            made.append(
                pltpu.make_async_remote_copy(
                    src_ref=src.at[rs, cs],
                    dst_ref=dst.at[rd, cd],
                    send_sem=surf_send.at[i, n],
                    recv_sem=surf_recv.at[i, m],
                    device_id=(x + b, y + c, z),
                    device_id_type=MESH,
                )
            )
        return made

    def surf_start(b, c):
        for copy in surf_copies(b, c):
            copy.start()

    for o in surf_offsets:
        pl.when(surf_present(*o, False))(lambda o=o: surf_start(*o))

    tall, span = rows + 2 * STEPS, share + width
    row_at = x * rows - STEPS + lax.broadcasted_iota(jnp.int32, (tall, span), 0)
    lane_at = lax.broadcasted_iota(jnp.int32, (tall, span), 1)
    lane_at = jnp.where(lane_at >= span - width // 2, lane_at - span, lane_at)
    col_at = y * cols + z * share + lane_at
    inside[...] = jnp.where(
        (row_at >= 0) & (row_at < rows * nx) & (col_at >= 0) & (col_at < cols * ny), time_step, 0.0
    )

    cell_at = lax.broadcasted_iota(jnp.int32, (width, share), 0) * ratio_c
    col = z * share + lax.broadcasted_iota(jnp.int32, (width, share), 1)
    spreader[...] = jnp.where((col >= cell_at) & (col < cell_at + ratio_c), 1.0, 0.0).astype(jnp.bfloat16)
    for o in OFFSETS:
        pl.when(present(*o))(lambda o=o: rim_copy(*o).wait_send())
    for b, c in surf_offsets:

        def sent(b=b, c=c):
            for copy in surf_copies(b, c):
                copy.wait_send()

        pl.when(surf_present(b, c, False))(sent)

    for a, b, c in OFFSETS:
        pl.when(present(a, b, c))(lambda o=(-a, -b, -c): rim_copy(*o).wait_recv())
    from_low = sub < cells // 2
    from_left = (lane % 4) < 2
    for a in SIGNS:
        joined = []
        low = from_cols[(a + 1) * 3 + 1, 0]
        high = from_cols[(a + 1) * 3 + 1, 1]
        if True:
            joined.append(jnp.where(from_left, low, high))
            low = jnp.where(from_low, from_cols[(a + 1) * 3 + 2, 0], from_cols[(a + 1) * 3, 0])
            high = jnp.where(from_low, from_cols[(a + 1) * 3 + 2, 1], from_cols[(a + 1) * 3, 1])
            joined.append(jnp.where(from_left, low, high))
        for f in range(4):
            for d in range(depth) if a == 0 else (range(2) if a > 0 else range(depth - 2, depth)):
                layer = REACH + a * depth + d
                t, p = (d // 2) * 2 + f // 2, (d % 2) * 2 + f % 2
                if a == 0:
                    center, above, below = field[f, d], from_rows[0, t], from_rows[1, t]
                else:
                    center = from_depth[side(a), f, d % 2]
                    above = from_rows_depth[side(a), 0, f // 2]
                    below = from_rows_depth[side(a), 1, f // 2]
                above = pltpu.roll(above, 6 - 2 * p, 0) if p != 3 else above
                below = pltpu.roll(below, 8 - 2 * p, 0) if p else below
                j = f * depth + d
                ext[f, layer, 0:cells, 0:width] = center
                ext[f, layer, cells:, 0:width] = jnp.where(from_low, below, above)
                turn = (width - 2 - 4 * j) % width
                for r in range(2):
                    tile = pltpu.roll(joined[r], turn, 1) if turn else joined[r]
                    ext[f, layer, r * cells : (r + 1) * cells, width:] = tile

    wide = depth + 2 * REACH
    for d, k in enumerate(weighted(ext[3, d] for d in range(wide))):
        gain[d] = drag + W_ALL * ext[3, d + 1] + k
    m0 = m1 = jnp.zeros((cells, width), jnp.float32)
    for f in range(3):
        for d, k in enumerate(weighted(ext[f, d] for d in range(wide))):
            image[f, d] = gain[d] * ext[f, d + 1] - ext[3, d + 1] * k
        for d, k in enumerate(weighted(ext[3, d] * ext[f, d] for d in range(wide))):
            out = jnp.where(ext[3, d + 1] > 0.0, image[f, d] - k, 0.0)
            image[f, d] = out
            if 0 < d <= depth:
                b = field[f, d - 1]
                m0 = m0 + b * b
                m1 = m1 + b * out[0:cells, 0:width]
    m0, m1 = total(m0), total(m1)
    own = jnp.where(m0 > 0.0, m1 / m0, 0.0)
    for f in range(3):
        for d, k in enumerate(weighted(image[f, d] for d in range(wide - 2))):
            ab = image[f, d + 1, 0:cells, 0:width]
            again[f, d] = gain[d + 1, 0:cells, 0:width] * ab - field[3, d] * k[0:cells, 0:width]
        for d, k in enumerate(weighted(ext[3, d + 1] * image[f, d] for d in range(wide - 2))):
            again[f, d] = again[f, d] - k[0:cells, 0:width]
    sums = [jnp.zeros((cells, width), jnp.float32) for _ in range(4)]
    for f in range(3):
        for d in range(depth):
            b = field[f, d]
            ab = image[f, d + 1, 0:cells, 0:width]
            w = ab - own * b
            aw = again[f, d] - own * ab
            for i, (p, q) in enumerate(((w, b), (w, w), (w, aw), (b, aw))):
                sums[i] = sums[i] + p * q
    numbers = [m0, m1, own] + [total(s) for s in sums]
    spot = lax.broadcasted_iota(jnp.int32, (1, width), 1)
    line = jnp.zeros((1, width), jnp.float32)
    for i, number in enumerate(numbers):
        line = jnp.where(spot == i, number, line)
    row_out[0] = line
    me = (x * ny + y) * nz + z
    gathered[me] = line
    top_own[0] = field[2, depth - 1]
    top_own[1] = image[2, depth, 0:cells, 0:width]
    for a, b, c in others:
        pltpu.make_async_remote_copy(
            src_ref=row_out.at[0],
            dst_ref=gathered.at[me],
            send_sem=sum_send,
            recv_sem=sum_recv,
            device_id=(xs[a], ys[b], zs[c]),
            device_id_type=MESH,
        ).start()

    def top_copy(k):
        return pltpu.make_async_remote_copy(
            src_ref=top_own,
            dst_ref=top_in,
            send_sem=top_send.at[k],
            recv_sem=top_recv,
            device_id=(x, y, zs[k]),
            device_id_type=MESH,
        )

    @pl.when(is_top)
    def _():
        for k in range(1, nz):
            top_copy(k).start()

    for b, c in surf_offsets:

        def arrived(b=b, c=c):
            for copy in surf_copies(-b, -c):
                copy.wait_recv()

        pl.when(surf_present(b, c, True))(arrived)
    loads[3].wait()
    start = pl.multiple_of(z * share, share)
    left_half = lax.broadcasted_iota(jnp.int32, (1, width), 1) < width // 2

    def joined_window(ref):
        wide = ref[:, pl.ds(start, share + 2 * width)].astype(jnp.float32)
        rim = jnp.where(left_half, wide[:, width + share :], wide[:, :width])
        return jnp.concatenate([wide[:, width : width + share], rim], axis=1)

    work[...] = joined_window(height)
    k = joined_window(conduct)[krow - STEPS : krow + rows + STEPS]
    face_right[...] = 0.5 * (k + pltpu.roll(k, span - 1, 1))
    face_down[...] = 0.5 * (k + pltpu.roll(k, tall - 1, 0))
    def stepped():
        h = work[...]
        s = pltpu.roll(h, span - 1, 1) - h
        along = face_right[...] * s * lax.rsqrt(1.0 + s * s)
        s = pltpu.roll(h, tall - 1, 0) - h
        across = face_down[...] * s * lax.rsqrt(1.0 + s * s)
        change = along - pltpu.roll(along, 1, 1) + across - pltpu.roll(across, 1, 0)
        return h + inside[...] * change

    def diffuse(_, carry):
        for _ in range(2):
            work[...] = stepped()
        return carry

    lax.fori_loop(0, (STEPS - 1) // 2, diffuse, 0)
    for _ in range((STEPS - 1) % 2):
        work[...] = stepped()
    surface_ref[...] = stepped()[STEPS : STEPS + rows, 0:share]

    @pl.when(jnp.logical_not(is_top))
    def _():
        top_copy(1).wait_recv()
        top_own[...] = top_in[...]

    spread = picked(top_own[...].reshape(2 * cells, width), spreader[...])

    @pl.when(is_top)
    def _():
        for k in range(1, nz):
            top_copy(k).wait_send()

    most = gathered.at[pl.ds(0, count - 1)]
    pltpu.make_async_copy(most, most, sum_send).wait()
    pltpu.make_async_copy(most, most, sum_recv).wait()

    table = gathered[...].reshape(count, width)
    m0, m1, own, e, ww, waw, baw = [table[:, i : i + 1] for i in range(7)]
    rr = m0.sum(axis=0, keepdims=True)
    bab = m1.sum(axis=0, keepdims=True)
    mean = bab / rr
    off = own - mean
    s2 = (ww + off * (2.0 * e + off * m0)).sum(axis=0, keepdims=True)
    q = (waw + off * (ww + own * e + baw + off * m1)).sum(axis=0, keepdims=True)
    alpha0 = rr / bab
    beta = s2 / (mean * bab)
    alpha1 = s2 / (q - s2 * s2 / bab)
    on_b = alpha0 + alpha1 * (1.0 + beta)
    on_ab = -alpha1 * alpha0
    for f in range(3):
        velocity_ref[f] = on_b * field[f] + on_ab * image[f, 1:-1, 0:cells, 0:width]
    rise = (STEPS * time_step) * (on_b * spread[:cells] + on_ab * spread[cells:])
    rise = jnp.broadcast_to(rise[:, None, :], (cells, ratio_r, share)).reshape(rows, share)
    surface_ref[...] = surface_ref[...] + rise


def local(sizes, body_force, viscosity, topography, kappa):
    depth, cells, width = viscosity.shape
    rows, cols = topography.shape
    nx, ny, nz = sizes
    count = nx * ny * nz
    share = cols // nz
    f32 = jnp.float32
    dma = pltpu.SemaphoreType.DMA
    return pl.pallas_call(
        functools.partial(kernel, sizes),
        out_shape=(
            jax.ShapeDtypeStruct(body_force.shape, f32),
            jax.ShapeDtypeStruct((rows, share), f32),
        ),
        in_specs=[pl.BlockSpec(memory_space=pltpu.HBM)] * 4,
        out_specs=[pl.BlockSpec(memory_space=pltpu.VMEM)] * 2,
        scratch_shapes=[
            pltpu.VMEM((4, depth, cells, width), f32),
            pltpu.VMEM((cells, width), f32),
            pltpu.VMEM((2, depth, cells, width), f32),
            pltpu.VMEM((2, 4, REACH, cells, width), f32),
            pltpu.VMEM((2, depth, cells, width), f32),
            pltpu.VMEM((2, 2, 2, cells, width), f32),
            pltpu.VMEM((9, 2, cells, width), f32),
            pltpu.VMEM((4, depth + 2 * REACH, 2 * cells, 2 * width), f32),
            pltpu.VMEM((3, depth + 2 * REACH - 2, 2 * cells, 2 * width), f32),
            pltpu.VMEM((depth + 2 * REACH - 2, 2 * cells, 2 * width), f32),
            pltpu.VMEM((3, depth, cells, width), f32),
            pltpu.VMEM((width, share), jnp.bfloat16),
            pltpu.VMEM((rows + 2 * STEPS, cols + 2 * width), f32),
            pltpu.VMEM((rows + 32, cols + 2 * width), kappa.dtype),
            pltpu.VMEM((rows + 2 * STEPS, share + width), f32),
            pltpu.VMEM((rows + 2 * STEPS, share + width), f32),
            pltpu.VMEM((rows + 2 * STEPS, share + width), f32),
            pltpu.VMEM((rows + 2 * STEPS, share + width), f32),
            pltpu.VMEM((1, 1, width), f32),
            pltpu.VMEM((count, 1, width), f32),
            pltpu.VMEM((2, cells, width), f32),
            pltpu.VMEM((2, cells, width), f32),
            dma((4,)),
            dma((27,)),
            dma((27,)),
            dma((2, 9)),
            dma((2, 9)),
            dma,
            dma,
            dma((nz,)),
            dma,
        ],
        compiler_params=pltpu.CompilerParams(
            collective_id=0, has_side_effects=True, vmem_limit_bytes=32 * 1024 * 1024
        ),
    )(*[pltpu.with_memory_space_constraint(one, pltpu.HBM) for one in (body_force, viscosity, topography, kappa)])


def solution(mesh):
    sizes = tuple(mesh.shape[axis] for axis in ("gx", "gy", "gz"))
    in_specs = (P(None, "gz", "gx", "gy"), P("gz", "gx", "gy"), P("gx", "gy"), P("gx", "gy"))
    out_specs = (P(None, "gz", "gx", "gy"), P("gx", ("gy", "gz")))
    return jax.shard_map(
        functools.partial(local, sizes), mesh=mesh, in_specs=in_specs, out_specs=out_specs, check_vma=False
    )
```

```python
import functools

import jax
import jax.numpy as jnp
from jax import lax
from jax.experimental import pallas as pl
from jax.experimental.pallas import tpu as pltpu
from jax.sharding import PartitionSpec as P

STEPS = 8
REACH = 2

drag = 1.0
time_step = 1.0
load_gain = 4.0

W_FACE = 0.5
W_EDGE = 0.25
W_CORNER = 0.5 / 3.0
W_ALL = 6 * W_FACE + 12 * W_EDGE + 8 * W_CORNER

MESH = pl.DeviceIdType.MESH
SIGNS = (-1, 0, 1)
OFFSETS = sorted(
    [(a, b, c) for a in SIGNS for b in SIGNS for c in SIGNS if (a, b, c) != (0, 0, 0)],
    key=lambda o: (abs(o[0]) + abs(o[1]) + abs(o[2]), abs(o[2])),
)


def side(sign):
    return 0 if sign < 0 else 1


def code(a, b, c):
    return (a + 1) * 9 + (b + 1) * 3 + (c + 1)


def partner(at, k, size):
    if size & (size - 1):
        return lax.rem(at + k, size)
    bit = 1
    moved = at
    while bit < size:
        if k & bit:
            moved = moved + bit * (1 - 2 * lax.rem(lax.div(at, bit), 2))
        bit *= 2
    return moved


def weighted(layers):
    held = []
    for u in layers:
        rows, lanes = u.shape
        beside = pltpu.roll(u, 1, 1) + pltpu.roll(u, lanes - 1, 1)
        held.append((W_FACE * beside, W_FACE * u + W_EDGE * beside, W_EDGE * u + W_CORNER * beside))
        if len(held) == 3:
            (_, near0, far0), (level, near1, _), (_, near2, far2) = held
            level = level + (near0 + near2)
            next_row = near1 + (far0 + far2)
            yield level + (pltpu.roll(next_row, 1, 0) + pltpu.roll(next_row, rows - 1, 0))
            held.pop(0)


def picked(x, choice):
    parts = []
    for _ in range(3):
        part = x.astype(jnp.bfloat16)
        parts.append(part.astype(jnp.float32))
        x = x - parts[-1]
    rows = x.shape[0]
    stacked = jnp.concatenate(parts, axis=0).astype(jnp.bfloat16)
    out = jnp.dot(stacked, choice, preferred_element_type=jnp.float32)
    return out[:rows] + (out[rows : 2 * rows] + out[2 * rows :])


def total(x):
    return x.sum(axis=(0, 1), keepdims=True)


def kernel(
    sizes,
    force_hbm,
    visc_hbm,
    topo_hbm,
    kappa_hbm,
    velocity_ref,
    surface_ref,
    field,
    lane_pack,
    row_pack,
    from_depth,
    from_rows,
    from_rows_depth,
    from_cols,
    ext,
    image,
    gain,
    again,
    spreader,
    height,
    conduct,
    work,
    face_right,
    face_down,
    inside,
    row_out,
    gathered,
    top_own,
    top_in,
    load_sem,
    rim_send,
    rim_recv,
    surf_send,
    surf_recv,
    sum_send,
    sum_recv,
    top_send,
    top_recv,
):
    nx, ny, nz = sizes
    count = nx * ny * nz
    x, y, z = lax.axis_index("gx"), lax.axis_index("gy"), lax.axis_index("gz")
    depth, cells, width = field.shape[1:]
    rows, cols = topo_hbm.shape
    share = cols // nz
    krow = 16

    xs = [partner(x, k, nx) for k in range(nx)]
    ys = [partner(y, k, ny) for k in range(ny)]
    zs = [partner(z, k, nz) for k in range(nz)]
    others = [(a, b, c) for a in range(nx) for b in range(ny) for c in range(nz)][1:]
    others.sort(key=lambda o: -(o[0] // 2 + o[1] + o[2]))
    is_top = z == nz - 1

    loads = [
        pltpu.make_async_copy(topo_hbm, height.at[STEPS : STEPS + rows, width : width + cols], load_sem.at[0]),
        pltpu.make_async_copy(force_hbm, field.at[0:3], load_sem.at[1]),
        pltpu.make_async_copy(visc_hbm, field.at[3], load_sem.at[2]),
        pltpu.make_async_copy(kappa_hbm, conduct.at[krow : krow + rows, width : width + cols], load_sem.at[3]),
    ]
    for copy in loads:
        copy.start()

    for ref in (from_depth, from_rows, from_rows_depth, from_cols):
        ref[...] = jnp.zeros_like(ref)
    height[0:STEPS, :] = jnp.zeros((STEPS, height.shape[1]), height.dtype)
    height[STEPS + rows :, :] = jnp.zeros((STEPS, height.shape[1]), height.dtype)
    height[STEPS : STEPS + rows, 0:width] = jnp.zeros((rows, width), height.dtype)
    height[STEPS : STEPS + rows, width + cols :] = jnp.zeros((rows, width), height.dtype)
    conduct[0:krow, :] = jnp.zeros((krow, conduct.shape[1]), conduct.dtype)
    conduct[krow + rows :, :] = jnp.zeros((krow, conduct.shape[1]), conduct.dtype)
    conduct[krow : krow + rows, 0:width] = jnp.zeros((rows, width), conduct.dtype)
    conduct[krow : krow + rows, width + cols :] = jnp.zeros((rows, width), conduct.dtype)

    barrier = pltpu.get_barrier_semaphore()
    for a, b, c in reversed(others):
        pl.semaphore_signal(barrier, inc=1, device_id=(xs[a], ys[b], zs[c]), device_id_type=MESH)

    ratio_r, ratio_c = rows // cells, cols // width
    at = lax.broadcasted_iota(jnp.int32, (cols, width), 0)
    first = lax.broadcasted_iota(jnp.int32, (cols, width), 1) * ratio_c
    pick = jnp.where((at >= first) & (at < first + ratio_c), 1.0, 0.0).astype(jnp.bfloat16)

    def present(a, b, c):
        yes = None
        for sign, at_, size in ((a, z, nz), (b, x, nx), (c, y, ny)):
            if sign:
                one = at_ > 0 if sign < 0 else at_ < size - 1
                yes = one if yes is None else jnp.logical_and(yes, one)
        return yes

    loads[1].wait()
    loads[2].wait()
    lane = lax.broadcasted_iota(jnp.int32, (cells, width), 1)
    sub = lax.broadcasted_iota(jnp.int32, (cells, width), 0)

    def in_lane_pack(f, d, tile, packed):
        j = f * depth + d
        return jnp.where((lane >= 4 * j) & (lane < 4 * j + 4), pltpu.roll(tile, (4 * j + 2) % width, 1), packed)

    def in_row_pack(f, d, tile, packed, first_row):
        p = (d % 2) * 2 + f % 2
        turn = (2 * p - first_row) % cells
        return jnp.where((sub >= 2 * p) & (sub < 2 * p + 2), pltpu.roll(tile, turn, 0) if turn else tile, packed)

    packed = jnp.zeros((cells, width), jnp.float32)
    for f in range(4):
        for d in range(depth):
            packed = in_lane_pack(f, d, field[f, d], packed)
    for t in range(depth):
        for i, first_row in enumerate((0, cells - 2)):
            rim = jnp.zeros((cells, width), jnp.float32)
            for d in (t // 2 * 2, t // 2 * 2 + 1):
                for f in (t % 2 * 2, t % 2 * 2 + 1):
                    rim = in_row_pack(f, d, field[f, d], rim, first_row)
            row_pack[i, t] = rim

    loads[0].wait()
    by_rows = height[STEPS : STEPS + rows, width : width + cols].reshape(cells, ratio_r, cols).sum(axis=1)
    load = picked(by_rows, pick) * (1.0 / (ratio_r * ratio_c))
    loaded = field[2, depth - 1] + jnp.where(is_top, -load_gain * load, 0.0)
    field[2, depth - 1] = loaded
    lane_pack[...] = in_lane_pack(2, depth - 1, loaded, packed)
    for i, first_row in enumerate((0, cells - 2)):
        row_pack[i, depth - 1] = in_row_pack(2, depth - 1, loaded, row_pack[i, depth - 1], first_row)

    def rim_copy(a, b, c):
        span = slice(depth - 2, depth) if a > 0 else slice(0, 2)
        if c != 0:
            src, dst = lane_pack, from_cols.at[(1 - a) * 3 + (1 - b), side(-c)]
        elif b == 0:
            src, dst = field.at[:, span], from_depth.at[side(-a)]
        elif a == 0:
            src, dst = row_pack.at[side(b)], from_rows.at[side(-b)]
        else:
            src, dst = row_pack.at[side(b), span], from_rows_depth.at[side(-a), side(-b)]
        return pltpu.make_async_remote_copy(
            src_ref=src,
            dst_ref=dst,
            send_sem=rim_send.at[code(a, b, c)],
            recv_sem=rim_recv.at[code(-a, -b, -c)],
            device_id=(x + b, y + c, z + a),
            device_id_type=MESH,
        )

    pl.semaphore_wait(barrier, count - 1)
    for o in OFFSETS:
        pl.when(present(*o))(lambda o=o: rim_copy(*o).start())

    surf_offsets = [(b, c) for b in SIGNS for c in SIGNS if (b, c) != (0, 0)]

    def surf_present(b, c, receiving):
        yes = present(0, b, c)
        toward = -c if receiving else c
        if toward > 0:
            yes = jnp.logical_and(yes, z == 0)
        if toward < 0:
            yes = jnp.logical_and(yes, z == nz - 1)
        return yes

    def surf_copies(b, c):
        def spans(sign, size, halo, lead):
            if sign == 0:
                return slice(0, size), slice(lead, lead + size)
            if sign > 0:
                return slice(size - halo, size), slice(0, halo)
            return slice(0, halo), slice(lead + size, lead + size + halo)

        cs, cd = spans(c, cols, width, width)
        n = (b + 1) * 3 + (c + 1)
        m = (1 - b) * 3 + (1 - c)
        made = []
        for i, (src, dst, halo) in enumerate(((topo_hbm, height, STEPS), (kappa_hbm, conduct, krow))):
            rs, rd = spans(b, rows, halo, halo)
            made.append(
                pltpu.make_async_remote_copy(
                    src_ref=src.at[rs, cs],
                    dst_ref=dst.at[rd, cd],
                    send_sem=surf_send.at[i, n],
                    recv_sem=surf_recv.at[i, m],
                    device_id=(x + b, y + c, z),
                    device_id_type=MESH,
                )
            )
        return made

    def surf_start(b, c):
        for copy in surf_copies(b, c):
            copy.start()

    for o in surf_offsets:
        pl.when(surf_present(*o, False))(lambda o=o: surf_start(*o))

    tall, span = rows + 2 * STEPS, share + width
    row_at = x * rows - STEPS + lax.broadcasted_iota(jnp.int32, (tall, span), 0)
    lane_at = lax.broadcasted_iota(jnp.int32, (tall, span), 1)
    lane_at = jnp.where(lane_at >= span - width // 2, lane_at - span, lane_at)
    col_at = y * cols + z * share + lane_at
    inside[...] = jnp.where(
        (row_at >= 0) & (row_at < rows * nx) & (col_at >= 0) & (col_at < cols * ny), time_step, 0.0
    )

    cell_at = lax.broadcasted_iota(jnp.int32, (width, share), 0) * ratio_c
    col = z * share + lax.broadcasted_iota(jnp.int32, (width, share), 1)
    spreader[...] = jnp.where((col >= cell_at) & (col < cell_at + ratio_c), 1.0, 0.0).astype(jnp.bfloat16)
    for o in OFFSETS:
        pl.when(present(*o))(lambda o=o: rim_copy(*o).wait_send())
    for b, c in surf_offsets:

        def sent(b=b, c=c):
            for copy in surf_copies(b, c):
                copy.wait_send()

        pl.when(surf_present(b, c, False))(sent)

    for a, b, c in OFFSETS:
        pl.when(present(a, b, c))(lambda o=(-a, -b, -c): rim_copy(*o).wait_recv())
    from_low = sub < cells // 2
    from_left = (lane % 4) < 2
    for a in SIGNS:
        joined = []
        low = from_cols[(a + 1) * 3 + 1, 0]
        high = from_cols[(a + 1) * 3 + 1, 1]
        if True:
            joined.append(jnp.where(from_left, low, high))
            low = jnp.where(from_low, from_cols[(a + 1) * 3 + 2, 0], from_cols[(a + 1) * 3, 0])
            high = jnp.where(from_low, from_cols[(a + 1) * 3 + 2, 1], from_cols[(a + 1) * 3, 1])
            joined.append(jnp.where(from_left, low, high))
        for f in range(4):
            for d in range(depth) if a == 0 else (range(2) if a > 0 else range(depth - 2, depth)):
                layer = REACH + a * depth + d
                t, p = (d // 2) * 2 + f // 2, (d % 2) * 2 + f % 2
                if a == 0:
                    center, above, below = field[f, d], from_rows[0, t], from_rows[1, t]
                else:
                    center = from_depth[side(a), f, d % 2]
                    above = from_rows_depth[side(a), 0, f // 2]
                    below = from_rows_depth[side(a), 1, f // 2]
                above = pltpu.roll(above, 6 - 2 * p, 0) if p != 3 else above
                below = pltpu.roll(below, 8 - 2 * p, 0) if p else below
                j = f * depth + d
                ext[f, layer, 0:cells, 0:width] = center
                ext[f, layer, cells:, 0:width] = jnp.where(from_low, below, above)
                turn = (width - 2 - 4 * j) % width
                for r in range(2):
                    tile = pltpu.roll(joined[r], turn, 1) if turn else joined[r]
                    ext[f, layer, r * cells : (r + 1) * cells, width:] = tile

    wide = depth + 2 * REACH
    for d, k in enumerate(weighted(ext[3, d] for d in range(wide))):
        gain[d] = drag + W_ALL * ext[3, d + 1] + k
    m0 = m1 = jnp.zeros((cells, width), jnp.float32)
    for f in range(3):
        for d, k in enumerate(weighted(ext[f, d] for d in range(wide))):
            image[f, d] = gain[d] * ext[f, d + 1] - ext[3, d + 1] * k
        for d, k in enumerate(weighted(ext[3, d] * ext[f, d] for d in range(wide))):
            out = jnp.where(ext[3, d + 1] > 0.0, image[f, d] - k, 0.0)
            image[f, d] = out
            if 0 < d <= depth:
                b = field[f, d - 1]
                m0 = m0 + b * b
                m1 = m1 + b * out[0:cells, 0:width]
    m0, m1 = total(m0), total(m1)
    own = jnp.where(m0 > 0.0, m1 / m0, 0.0)
    for f in range(3):
        for d, k in enumerate(weighted(image[f, d] for d in range(wide - 2))):
            ab = image[f, d + 1, 0:cells, 0:width]
            again[f, d] = gain[d + 1, 0:cells, 0:width] * ab - field[3, d] * k[0:cells, 0:width]
        for d, k in enumerate(weighted(ext[3, d + 1] * image[f, d] for d in range(wide - 2))):
            again[f, d] = again[f, d] - k[0:cells, 0:width]
    sums = [jnp.zeros((cells, width), jnp.float32) for _ in range(4)]
    for f in range(3):
        for d in range(depth):
            b = field[f, d]
            ab = image[f, d + 1, 0:cells, 0:width]
            w = ab - own * b
            aw = again[f, d] - own * ab
            for i, (p, q) in enumerate(((w, b), (w, w), (w, aw), (b, aw))):
                sums[i] = sums[i] + p * q
    numbers = [m0, m1, own] + [total(s) for s in sums]
    spot = lax.broadcasted_iota(jnp.int32, (1, width), 1)
    line = jnp.zeros((1, width), jnp.float32)
    for i, number in enumerate(numbers):
        line = jnp.where(spot == i, number, line)
    row_out[0] = line
    me = (x * ny + y) * nz + z
    gathered[me] = line
    top_own[0] = field[2, depth - 1]
    top_own[1] = image[2, depth, 0:cells, 0:width]
    for a, b, c in others:
        pltpu.make_async_remote_copy(
            src_ref=row_out.at[0],
            dst_ref=gathered.at[me],
            send_sem=sum_send,
            recv_sem=sum_recv,
            device_id=(xs[a], ys[b], zs[c]),
            device_id_type=MESH,
        ).start()

    def top_copy(k):
        return pltpu.make_async_remote_copy(
            src_ref=top_own,
            dst_ref=top_in,
            send_sem=top_send.at[k],
            recv_sem=top_recv,
            device_id=(x, y, zs[k]),
            device_id_type=MESH,
        )

    @pl.when(is_top)
    def _():
        for k in range(1, nz):
            top_copy(k).start()

    for b, c in surf_offsets:

        def arrived(b=b, c=c):
            for copy in surf_copies(-b, -c):
                copy.wait_recv()

        pl.when(surf_present(b, c, True))(arrived)
    loads[3].wait()
    start = pl.multiple_of(z * share, share)
    left_half = lax.broadcasted_iota(jnp.int32, (1, width), 1) < width // 2

    def joined_window(ref):
        wide = ref[:, pl.ds(start, share + 2 * width)].astype(jnp.float32)
        rim = jnp.where(left_half, wide[:, width + share :], wide[:, :width])
        return jnp.concatenate([wide[:, width : width + share], rim], axis=1)

    work[...] = joined_window(height)
    k = joined_window(conduct)[krow - STEPS : krow + rows + STEPS]
    face_right[...] = 0.5 * (k + pltpu.roll(k, span - 1, 1))
    face_down[...] = 0.5 * (k + pltpu.roll(k, tall - 1, 0))
    def stepped():
        h = work[...]
        s = pltpu.roll(h, span - 1, 1) - h
        along = face_right[...] * s * lax.rsqrt(1.0 + s * s)
        s = pltpu.roll(h, tall - 1, 0) - h
        across = face_down[...] * s * lax.rsqrt(1.0 + s * s)
        change = along - pltpu.roll(along, 1, 1) + across - pltpu.roll(across, 1, 0)
        return h + inside[...] * change

    def diffuse(_, carry):
        for _ in range(2):
            work[...] = stepped()
        return carry

    lax.fori_loop(0, (STEPS - 1) // 2, diffuse, 0)
    for _ in range((STEPS - 1) % 2):
        work[...] = stepped()
    surface_ref[...] = stepped()[STEPS : STEPS + rows, 0:share]

    @pl.when(jnp.logical_not(is_top))
    def _():
        top_copy(1).wait_recv()
        top_own[...] = top_in[...]

    spread = picked(top_own[...].reshape(2 * cells, width), spreader[...])

    @pl.when(is_top)
    def _():
        for k in range(1, nz):
            top_copy(k).wait_send()

    most = gathered.at[pl.ds(0, count - 1)]
    pltpu.make_async_copy(most, most, sum_send).wait()
    pltpu.make_async_copy(most, most, sum_recv).wait()

    table = gathered[...].reshape(count, width)
    m0, m1, own, e, ww, waw, baw = [table[:, i : i + 1] for i in range(7)]
    rr = m0.sum(axis=0, keepdims=True)
    bab = m1.sum(axis=0, keepdims=True)
    mean = bab / rr
    off = own - mean
    s2 = (ww + off * (2.0 * e + off * m0)).sum(axis=0, keepdims=True)
    q = (waw + off * (ww + own * e + baw + off * m1)).sum(axis=0, keepdims=True)
    alpha0 = rr / bab
    beta = s2 / (mean * bab)
    alpha1 = s2 / (q - s2 * s2 / bab)
    on_b = alpha0 + alpha1 * (1.0 + beta)
    on_ab = -alpha1 * alpha0
    for f in range(3):
        velocity_ref[f] = on_b * field[f] + on_ab * image[f, 1:-1, 0:cells, 0:width]
    rise = (STEPS * time_step) * (on_b * spread[:cells] + on_ab * spread[cells:])
    rise = jnp.broadcast_to(rise[:, None, :], (cells, ratio_r, share)).reshape(rows, share)
    surface_ref[...] = surface_ref[...] + rise


def local(sizes, body_force, viscosity, topography, kappa):
    depth, cells, width = viscosity.shape
    rows, cols = topography.shape
    nx, ny, nz = sizes
    count = nx * ny * nz
    share = cols // nz
    f32 = jnp.float32
    dma = pltpu.SemaphoreType.DMA
    return pl.pallas_call(
        functools.partial(kernel, sizes),
        out_shape=(
            jax.ShapeDtypeStruct(body_force.shape, f32),
            jax.ShapeDtypeStruct((rows, share), f32),
        ),
        in_specs=[pl.BlockSpec(memory_space=pltpu.HBM)] * 4,
        out_specs=[pl.BlockSpec(memory_space=pltpu.VMEM)] * 2,
        scratch_shapes=[
            pltpu.VMEM((4, depth, cells, width), f32),
            pltpu.VMEM((cells, width), f32),
            pltpu.VMEM((2, depth, cells, width), f32),
            pltpu.VMEM((2, 4, REACH, cells, width), f32),
            pltpu.VMEM((2, depth, cells, width), f32),
            pltpu.VMEM((2, 2, 2, cells, width), f32),
            pltpu.VMEM((9, 2, cells, width), f32),
            pltpu.VMEM((4, depth + 2 * REACH, 2 * cells, 2 * width), f32),
            pltpu.VMEM((3, depth + 2 * REACH - 2, 2 * cells, 2 * width), f32),
            pltpu.VMEM((depth + 2 * REACH - 2, 2 * cells, 2 * width), f32),
            pltpu.VMEM((3, depth, cells, width), f32),
            pltpu.VMEM((width, share), jnp.bfloat16),
            pltpu.VMEM((rows + 2 * STEPS, cols + 2 * width), f32),
            pltpu.VMEM((rows + 32, cols + 2 * width), kappa.dtype),
            pltpu.VMEM((rows + 2 * STEPS, share + width), f32),
            pltpu.VMEM((rows + 2 * STEPS, share + width), f32),
            pltpu.VMEM((rows + 2 * STEPS, share + width), f32),
            pltpu.VMEM((rows + 2 * STEPS, share + width), f32),
            pltpu.VMEM((1, 1, width), f32),
            pltpu.VMEM((count, 1, width), f32),
            pltpu.VMEM((2, cells, width), f32),
            pltpu.VMEM((2, cells, width), f32),
            dma((4,)),
            dma((27,)),
            dma((27,)),
            dma((2, 9)),
            dma((2, 9)),
            dma,
            dma,
            dma((nz,)),
            dma,
        ],
        compiler_params=pltpu.CompilerParams(
            collective_id=0, has_side_effects=True, vmem_limit_bytes=32 * 1024 * 1024
        ),
    )(*[pltpu.with_memory_space_constraint(one, pltpu.HBM) for one in (body_force, viscosity, topography, kappa)])


def solution(mesh):
    sizes = tuple(mesh.shape[axis] for axis in ("gx", "gy", "gz"))
    in_specs = (P(None, "gz", "gx", "gy"), P("gz", "gx", "gy"), P("gx", "gy"), P("gx", "gy"))
    out_specs = (P(None, "gz", "gx", "gy"), P("gx", ("gy", "gz")))
    return jax.shard_map(
        functools.partial(local, sizes), mesh=mesh, in_specs=in_specs, out_specs=out_specs, check_vma=False
    )
```
